256 devices in a mesh: sec: 4 (over z_lo), head: 8 (over x, z_hi), req: 8 (over y, core).
Axes of the slice: x: 4, y: 4, z: 8 (z_hi: 2, z_lo: 4; z = z_hi * 4 + z_lo), core: 2. Of those that a mesh axis runs over, the one named last changes fastest.
Arguments:
- prompt_x: bfloat16 [4096, 16384], P('req', 'sec'), may hold values from -6 to 6
- w_kv: bfloat16 [16384, 2048], P('sec', 'head'), may hold values from -0.046875 to 0.046875
- queries: bfloat16 [16, 16384], P('req', 'head'), may hold values from -120 to 120
- cache: bfloat16 [16, 4096, 8, 256], P('req', 'sec', 'head'), may hold values from -5 to 5
- w_out: bfloat16 [16384, 16384], P('head', ('sec', 'req')), may hold values from -0.046875 to 0.046875
- blk_owner: int32 [256, 1], replicated, may hold values from 0 to 7; in each aligned block of 8 rows (0 to 7, 8 to 15, ...) at most 2 rows name the same one
- blk_slot: int32 [256], replicated, may hold values from 0 to 1
- blk_len: int32 [256], replicated, may hold values from 1 to 16
- ctx_len: int32 [16], P('req'), may hold values from 2 to 4096
Outputs:
- projected: bfloat16 [16, 16384], P('head', ('sec', 'req'))
The draws below stay inside these ranges and needn't reach their ends.
Inputs may be any that keep to these rules, and one draw needn't show every extreme that they name: `blk_owner`: in each aligned run of 8 blocks (the blocks of one device) no owner is named more than 2 times, a bound that some block reaches.
All inputs are finite; a program needn't handle non-finite values.
Results may differ from the reference program's by a relative error of at most 0.013.
Values may be sent and summed in bfloat16 or wider, within the bound.
No kernel may reach another device: no remote copies, remote signals or barrier semaphores. Data moves between devices by JAX's collectives and lax.ppermute only.
A program may use at most 64 MiB of HBM per device.

```python
import math
import jax
import jax.numpy as jnp
import numpy as np
from jax import lax

D = 16384
HD = 128
QH = 128
KVH = 8
BLK = 16
CAP = 2
REQ_DEV = 2
PTOK = 4096
NB_DEV = 8
NBLK = 256
NREQ = 16
CTX = 4096
N_REQ = 8


def common_cache(key):
    return jnp.clip(jax.random.normal(key, (NREQ, CTX, KVH, 2 * HD), jnp.float32), -5.0, 5.0)


def draw_cache(key, part):
    values = common_cache(key)
    return values.astype(jnp.bfloat16)


def draw_queries(key, part):
    key = jax.random.fold_in(key, 202)
    base = jnp.clip(jax.random.normal(key, (NREQ, QH * HD), jnp.float32), -5.0, 5.0)
    return base.astype(jnp.bfloat16)


def place_ends(drawn, own_key, low, largest):
    shape = drawn.shape
    place = [jax.random.randint(jax.random.fold_in(own_key, axis), (), 0, shape[axis]) for axis in range(len(shape))]
    drawn = drawn.at[tuple(place)].set(low)
    longest = shape.index(max(shape))
    place[longest] = (place[longest] + 1) % shape[longest]
    return drawn.at[tuple(place)].set(largest)


def block_scale(key, shape, shards, smallest, largest):
    gain, own = 1.0, jax.random.fold_in(key, 6)
    for position, blocks in shards:
        steps = jnp.exp(jax.random.uniform(jax.random.fold_in(own, position), (blocks,), jnp.float32, smallest / len(shards), largest / len(shards)))
        gain = gain * jnp.repeat(steps, shape[position] // blocks).reshape([-1 if axis == position else 1 for axis in range(len(shape))])
    return gain


def assign_block(own_key, own, number, rows, number_of, top, most, slope):
    order = jax.random.permutation(own_key, number_of)
    crowded, common = portions_of(number_of, rows * top, most, slope, True), portions_of(number_of, rows * top, most, slope, False)
    places = jnp.arange(number_of)

    def named(lengths, offset_by):
        used = int((lengths > 0).sum())
        fixed = max(1, used // 4)
        passed = fixed + (places - fixed + offset_by * (used - fixed)) % max(1, number_of - fixed)
        return jnp.zeros((number_of,), jnp.int32).at[order[jnp.where(places < fixed, places, passed)]].set(jnp.asarray(lengths, jnp.int32))

    lengths = jnp.where(number % 4 == 0, named(crowded, number // 4), named(common, number - number // 4 - 1))
    mixed = jax.random.permutation(jax.random.fold_in(own, 3), number_of)
    source_of, sink = mixed[0:number_of // 2 * 2:2], mixed[1:number_of // 2 * 2:2]
    margin = jnp.minimum(lengths[source_of] - 1, most - lengths[sink]) // 2
    margin = jnp.where((source_of == order[0]) | (sink == order[0]) | (lengths[sink] == 0), 0, jnp.maximum(margin, 0))
    passed = jax.random.randint(jax.random.fold_in(own, 4), (number_of // 2,), 0, 1 << 20) % (margin + 1)
    lengths = lengths.at[source_of].add(-passed).at[sink].add(passed)
    labels = jnp.searchsorted(jnp.cumsum(lengths), jnp.arange(rows * top), side="right").astype(jnp.int32)
    grid = labels.reshape(top, rows).T
    grid = grid[jax.random.permutation(jax.random.fold_in(own, 1), rows)]
    offset_by = jax.random.randint(jax.random.fold_in(own, 2), (rows, 1), 0, top)
    return jnp.take_along_axis(grid, (jnp.arange(top)[None, :] + offset_by) % top, axis=1)


def portions_of(count, total, bound, skew, full):
    loads = [(1 << 20) // math.isqrt(grade ** skew) + 1 for grade in range(1, count + 1)]
    largest = bound if full else min(bound, max(-(-total // count), total * loads[0] // sum(loads)))
    least = 1 if total - largest >= count - 1 else 0
    counts, spare = [largest] + [least] * (count - 1), total - largest - least * (count - 1)
    while spare > 0:
        movable = [i for i in range(1, count) if counts[i] < largest] or [i for i in range(1, count) if counts[i] < bound]
        mass, left = sum([loads[i] for i in movable]), spare
        for i in movable:
            more = min(bound - counts[i], max(1, left * loads[i] // mass), spare)
            counts[i] = counts[i] + more
            spare = spare - more
    return np.array(counts)


def centred(own_key, dims, width, reach, cuts=(), held_as=jnp.bfloat16):
    values = jax.random.normal(own_key, dims, jnp.float32) * width
    if len(cuts) > 0:
        values = block_scale(own_key, dims, cuts, -0.22, 0.18) * values
    return jnp.clip(values, min=-reach, max=reach).astype(held_as)


def setup_inputs(seed: int = 0) -> dict:
    arg_keys = jax.random.split(jax.random.key(seed), 10)
    prompt_x = centred(arg_keys[0], (PTOK, D), 1.0, 6.0, ((0, 8), (1, 4)))
    w_kv = centred(arg_keys[1], (D, KVH * 2 * HD), D ** -0.5, 0.046875, ((0, 4), (1, 8)))
    queries = draw_queries(jax.random.fold_in(arg_keys[9], 71), 0)
    cache = draw_cache(jax.random.fold_in(arg_keys[9], 71), 0)
    w_out = centred(arg_keys[4], (QH * HD, D), (QH * HD) ** -0.5, 0.046875, ((0, 8), (1, 32)))
    blk_owner_keys = jax.random.split(jax.random.fold_in(arg_keys[5], 1), NBLK // NB_DEV)
    blk_owner_turns = jax.random.permutation(jax.random.fold_in(arg_keys[5], 3), NBLK // NB_DEV)
    blk_owner = jax.vmap(lambda own, number: assign_block(jax.random.fold_in(arg_keys[5], 2), own, number, NB_DEV, N_REQ, 1, CAP, 2))(blk_owner_keys, blk_owner_turns).reshape((NBLK, 1))
    blk_slot = place_ends(jax.random.randint(arg_keys[6], (NBLK,), 0, REQ_DEV), jax.random.fold_in(arg_keys[6], 1), 0, REQ_DEV - 1).astype(jnp.int32)
    blk_len = place_ends(jax.random.randint(arg_keys[7], (NBLK,), 1, BLK + 1), jax.random.fold_in(arg_keys[7], 1), 1, BLK).astype(jnp.int32)
    ctx_len = place_ends(jax.random.randint(arg_keys[8], (NREQ,), 2, CTX + 1), jax.random.fold_in(arg_keys[8], 1), 2, CTX).astype(jnp.int32)
    return dict(prompt_x=prompt_x, w_kv=w_kv, queries=queries, cache=cache, w_out=w_out, blk_owner=blk_owner, blk_slot=blk_slot, blk_len=blk_len, ctx_len=ctx_len)


def reference(prompt_x, w_kv, queries, cache, w_out, blk_owner, blk_slot, blk_len, ctx_len):
    new_kv = jnp.dot(prompt_x, w_kv, preferred_element_type=jnp.float32).astype(jnp.bfloat16)
    new_kv = new_kv.reshape(PTOK, KVH, 2 * HD).astype(jnp.float32)
    token_block = jnp.arange(PTOK, dtype=jnp.int32) // BLK
    token_place = jnp.arange(PTOK, dtype=jnp.int32) % BLK
    block_request = blk_owner[:, 0] * REQ_DEV + blk_slot
    owner_req = block_request[token_block]
    token_live = token_place < blk_len[token_block]
    new_keys = new_kv[:, :, :HD]
    new_values = new_kv[:, :, HD:]
    group = QH // KVH
    factor = 1.0 / math.sqrt(HD)
    positions = jnp.arange(CTX, dtype=jnp.int32)

    def one_request(index):
        query = lax.dynamic_index_in_dim(queries, index, 0, False).astype(jnp.float32).reshape(KVH, group, HD)
        stored = lax.dynamic_index_in_dim(cache, index, 0, False).astype(jnp.float32)
        length = lax.dynamic_index_in_dim(ctx_len, index, 0, False)
        cached_scores = jnp.einsum('kgd,pkd->kgp', query, stored[:, :, :HD]) * factor
        prompt_scores = jnp.einsum('kgd,tkd->kgt', query, new_keys) * factor
        cached_mask = positions < length
        prompt_mask = token_live & (owner_req == index)
        scores = jnp.concatenate([jnp.where(cached_mask[None, None, :], cached_scores, -jnp.inf), jnp.where(prompt_mask[None, None, :], prompt_scores, -jnp.inf)], axis=-1)
        weights = jax.nn.softmax(scores, axis=-1)
        result = jnp.einsum('kgp,pkd->kgd', weights[:, :, :CTX], stored[:, :, HD:])
        result = result + jnp.einsum('kgt,tkd->kgd', weights[:, :, CTX:], new_values)
        return result.reshape(QH * HD)
    attended = lax.map(one_request, jnp.arange(NREQ, dtype=jnp.int32)).astype(jnp.bfloat16)
    return jnp.dot(attended, w_out, preferred_element_type=jnp.float32).astype(jnp.bfloat16)
```

```python
import math

import jax
import jax.numpy as jnp
from jax import lax
from jax.experimental import pallas as pl
from jax.experimental.pallas import tpu as pltpu
from jax.sharding import PartitionSpec as P

HD = 128
BLK = 16
GROUP = 16
NREQ = 16
LANES = GROUP * NREQ
HALF = LANES // 2
STAT = 16
LOW = -1e30
FACTOR = 1.0 / math.sqrt(HD)
BF = jnp.bfloat16
F32 = jnp.float32


def vmem():
    return pl.BlockSpec(memory_space=pltpu.VMEM)


def smem():
    return pl.BlockSpec(memory_space=pltpu.SMEM)


def dot(a, b, dims):
    return lax.dot_general(a, b, (dims, ((), ())), preferred_element_type=F32)


def rows_of(queries):
    return jnp.concatenate([queries[:, h * HD : (h + 1) * HD] for h in range(GROUP)], axis=0)


def stat_rows(peak, total, rows):
    place = lax.broadcasted_iota(jnp.int32, (rows, peak.shape[1]), 0)
    return jnp.where(place == 0, peak, jnp.where(place == 1, total, 0.0))


def packed_stats(peak, total):
    hi = peak.astype(BF).astype(F32)
    rest = peak - hi
    mid = rest.astype(BF).astype(F32)
    low = rest - mid
    total_hi = total.astype(BF).astype(F32)
    total_low = total - total_hi
    place = lax.broadcasted_iota(jnp.int32, (STAT, peak.shape[1]), 0)
    packed = jnp.zeros((STAT, peak.shape[1]), F32)
    for row, part in enumerate((hi, mid, low, total_hi, total_low)):
        packed = jnp.where(place == row, part, packed)
    return packed.astype(BF)


def unpacked_stats(packed):
    rows = packed.astype(F32)
    peak = rows[0:1] + (rows[1:2] + rows[2:3])
    total = rows[3:4] + rows[4:5]
    return peak, total


def store_packed(ref, weighted, peak, total):
    ref[0:HD, :] = weighted.astype(BF)
    ref[HD : HD + STAT, :] = packed_stats(peak, total)


def cached_kernel(meta, q_ref, cache_ref, weighted_ref, stats_ref):
    queries = rows_of(q_ref[...])
    count = cache_ref.shape[1]
    lane = lax.broadcasted_iota(jnp.int32, (count, LANES), 1) % NREQ
    position = lax.broadcasted_iota(jnp.int32, (count, LANES), 0) + meta[18]
    first = meta[16] * 2
    live0 = (lane == first) & (position < meta[19])
    live1 = (lane == first + 1) & (position < meta[20])
    live = live0 | live1
    scores0 = dot(cache_ref[0, :, 0:HD], queries, ((1,), (1,)))
    scores1 = dot(cache_ref[1, :, 0:HD], queries, ((1,), (1,)))
    scores = jnp.where(live, jnp.where(lane == first, scores0, scores1) * FACTOR, LOW)
    peak = jnp.max(scores, axis=0, keepdims=True)
    weights = jnp.where(live, jnp.exp(scores - peak), 0.0)
    total = jnp.sum(weights, axis=0, keepdims=True)
    weights = weights.astype(BF)
    zero = jnp.zeros_like(weights)
    weighted_ref[...] = dot(
        cache_ref[0, :, HD : 2 * HD], jnp.where(live0, weights, zero), ((0,), (0,))
    ) + dot(cache_ref[1, :, HD : 2 * HD], jnp.where(live1, weights, zero), ((0,), (0,)))
    stats_ref[...] = stat_rows(peak, total, 8)


def prompt_kernel(
    meta, q_ref, perm_ref, own_ref, a_ref, b_ref, c_ref, cw_ref, cs_ref, kw_ref, ks_ref, send_ref
):
    summed = (own_ref[...].astype(F32) + a_ref[...].astype(F32)) + (
        b_ref[...].astype(F32) + c_ref[...].astype(F32)
    )
    new_kv = summed.astype(BF)
    ordered = dot(perm_ref[...], q_ref[...], ((1,), (0,))).astype(BF)
    queries = rows_of(ordered)
    scores = dot(new_kv[:, 0:HD], queries, ((1,), (1,))) * FACTOR
    tokens = new_kv.shape[0]
    lane = lax.broadcasted_iota(jnp.int32, (BLK, LANES), 1) % NREQ
    place = lax.broadcasted_iota(jnp.int32, (BLK, LANES), 0)
    pieces = []
    for block in range(tokens // BLK):
        live = (lane == meta[block]) & (place < meta[8 + block])
        pieces.append(jnp.where(live, scores[block * BLK : (block + 1) * BLK], LOW))
    scores = jnp.concatenate(pieces, axis=0)
    peak = jnp.max(scores, axis=0, keepdims=True)
    weights = jnp.where(scores > 0.5 * LOW, jnp.exp(scores - peak), 0.0)
    total = jnp.sum(weights, axis=0, keepdims=True)
    weighted = dot(new_kv[:, HD : 2 * HD], weights.astype(BF), ((0,), (0,)))
    cached_peak, cached_total = cs_ref[0:1, :], cs_ref[1:2, :]
    joint = jnp.maximum(peak, cached_peak)
    scale, cached_scale = jnp.exp(peak - joint), jnp.exp(cached_peak - joint)
    weighted = weighted * scale + cw_ref[...] * cached_scale
    total = total * scale + cached_total * cached_scale
    core = meta[17]

    @pl.when(core == 0)
    def _():
        kw_ref[...] = weighted[:, :HALF]
        ks_ref[...] = stat_rows(joint[:, :HALF], total[:, :HALF], 8)
        store_packed(send_ref, weighted[:, HALF:], joint[:, HALF:], total[:, HALF:])

    @pl.when(core == 1)
    def _():
        kw_ref[...] = weighted[:, HALF:]
        ks_ref[...] = stat_rows(joint[:, HALF:], total[:, HALF:], 8)
        store_packed(send_ref, weighted[:, :HALF], joint[:, :HALF], total[:, :HALF])


def joined(w_ref, s_ref, got_ref):
    peak, total = s_ref[0:1, :], s_ref[1:2, :]
    got_peak, got_total = unpacked_stats(got_ref[HD : HD + STAT, :])
    joint = jnp.maximum(peak, got_peak)
    scale, got_scale = jnp.exp(peak - joint), jnp.exp(got_peak - joint)
    weighted = w_ref[...] * scale + got_ref[0:HD, :].astype(F32) * got_scale
    return weighted, joint, total * scale + got_total * got_scale


def join_kernel(w_ref, s_ref, got_ref, kw_ref, ks_ref, send_ref):
    weighted, peak, total = joined(w_ref, s_ref, got_ref)
    kw_ref[...] = weighted
    ks_ref[...] = stat_rows(peak, total, 8)
    store_packed(send_ref, weighted, peak, total)


def last_kernel(w_ref, s_ref, got_ref, out_ref):
    weighted, peak, total = joined(w_ref, s_ref, got_ref)
    rows = (weighted / total).T
    for h in range(GROUP // 2):
        out_ref[:, h * HD : (h + 1) * HD] = rows[h * NREQ : (h + 1) * NREQ, :].astype(BF)


def shape(dims, dtype):
    return jax.ShapeDtypeStruct(dims, dtype)


def call(kernel, ins, outs, name, flops=0):
    moved = 0
    for _, value in ins:
        moved += value.size * value.dtype.itemsize
    return pl.pallas_call(
        kernel,
        out_shape=outs,
        in_specs=[spec for spec, _ in ins],
        out_specs=jax.tree.map(lambda _: vmem(), outs),
        compiler_params=pltpu.CompilerParams(vmem_limit_bytes=32 * 1024 * 1024),
        cost_estimate=pl.CostEstimate(flops=flops, bytes_accessed=moved, transcendentals=0),
        name=name,
    )(*[value for _, value in ins])


def joined_call(state, got, name):
    return call(
        join_kernel,
        [(vmem(), state[0]), (vmem(), state[1]), (vmem(), got)],
        (shape((HD, HALF), F32), shape((8, HALF), F32), shape((HD + STAT, HALF), BF)),
        name,
    )


def on_device(prompt_x, w_kv, queries, cache, w_out, blk_owner, blk_slot, blk_len, ctx_len):
    sec_count = lax.axis_size("sec")
    req_count = lax.axis_size("req")
    sec_id = lax.axis_index("sec")
    req_id = lax.axis_index("req")
    core = req_id % 2
    y_id = req_id // 2
    rows = prompt_x.shape[0] // sec_count

    def over_sec(value, flip):
        return lax.ppermute(value, "sec", [(i, i ^ flip) for i in range(sec_count)])

    def over_req(value, flip):
        return lax.ppermute(value, "req", [(i, i ^ flip) for i in range(req_count)])

    base = (req_id * sec_count + sec_id) * (rows // BLK)
    count = rows // BLK
    owner = lax.dynamic_slice(blk_owner, (base, 0), (count, 1))[:, 0]
    slot = lax.dynamic_slice(blk_slot, (base,), (count,))
    length = lax.dynamic_slice(blk_len, (base,), (count,))
    ids = jnp.stack([req_id, core, sec_id * cache.shape[1]]).astype(jnp.int32)
    meta = jnp.concatenate([owner * 2 + slot, length, ids, ctx_len]).astype(jnp.int32)

    gathered = queries
    for flip in (1, 2, 6):
        gathered = jnp.concatenate([gathered, over_req(gathered, flip)], axis=0)
    place = jnp.arange(NREQ, dtype=jnp.int32)
    member = place // 2
    holder = req_id ^ (member % 2) ^ ((member // 2) % 2 * 2) ^ (member // 4 * 6)
    perm = (holder[None, :] * 2 + place[None, :] % 2 == place[:, None]).astype(BF)

    part = jnp.dot(prompt_x, w_kv, preferred_element_type=F32).astype(BF)
    chunks = part.reshape(sec_count, rows, part.shape[1])

    def chunk(index):
        return lax.dynamic_index_in_dim(chunks, index, 0, False)

    arrived = [over_sec(chunk(sec_id ^ flip), flip) for flip in (3, 2, 1)]

    cached = call(
        cached_kernel,
        [
            (smem(), meta),
            (vmem(), jnp.tile(queries, (NREQ // 2, 1))),
            (vmem(), cache[:, :, 0, :]),
        ],
        (shape((HD, LANES), F32), shape((8, LANES), F32)),
        "cached",
        flops=2 * 4 * cache.shape[1] * HD * LANES,
    )
    state = call(
        prompt_kernel,
        [
            (smem(), meta),
            (vmem(), gathered),
            (vmem(), perm),
            (vmem(), chunk(sec_id)),
            (vmem(), arrived[0]),
            (vmem(), arrived[1]),
            (vmem(), arrived[2]),
            (vmem(), cached[0]),
            (vmem(), cached[1]),
        ],
        (shape((HD, HALF), F32), shape((8, HALF), F32), shape((HD + STAT, HALF), BF)),
        "prompt",
        flops=2 * 2 * rows * HD * LANES,
    )
    state = joined_call(state, over_req(state[2], 1), "join_core")
    state = joined_call(state, over_sec(state[2], 1), "join_sec1")
    state = joined_call(state, over_sec(state[2], 2), "join_sec2")
    state = joined_call(state, over_req(state[2], 2), "join_y1")
    got = over_req(state[2], 6)
    mine = call(
        last_kernel,
        [(vmem(), state[0]), (vmem(), state[1]), (vmem(), got)],
        shape((NREQ, HALF // NREQ * HD), BF),
        "join_y2",
    )
    other = over_req(mine, 1)
    attended = jnp.concatenate(
        [jnp.where(core == 0, mine, other), jnp.where(core == 0, other, mine)], axis=1
    )
    partial_out = jnp.dot(attended, w_out, preferred_element_type=F32).astype(BF)
    head_count = lax.axis_size("head")
    pieces = partial_out.reshape(head_count, NREQ // head_count, partial_out.shape[1])
    pieces = lax.all_to_all(pieces, "head", 0, 0, tiled=True)
    return jnp.sum(pieces.astype(F32), axis=0).astype(BF)


def solution(mesh):
    return jax.shard_map(
        on_device,
        mesh=mesh,
        in_specs=(
            P("req", "sec"),
            P("sec", "head"),
            P("req", "head"),
            P("req", "sec", "head", None),
            P("head", ("sec", "req")),
            P(),
            P(),
            P(),
            P("req"),
        ),
        out_specs=P("head", ("sec", "req")),
        check_vma=False,
    )
```

```python
import math

import jax
import jax.numpy as jnp
from jax import lax
from jax.experimental import pallas as pl
from jax.experimental.pallas import tpu as pltpu
from jax.sharding import PartitionSpec as P

HD = 128
BLK = 16
GROUP = 16
NREQ = 16
LANES = GROUP * NREQ
HALF = LANES // 2
STAT = 16
LOW = -1e30
FACTOR = 1.0 / math.sqrt(HD)
BF = jnp.bfloat16
F32 = jnp.float32


def vmem():
    return pl.BlockSpec(memory_space=pltpu.VMEM)


def smem():
    return pl.BlockSpec(memory_space=pltpu.SMEM)


def dot(a, b, dims):
    return lax.dot_general(a, b, (dims, ((), ())), preferred_element_type=F32)


def rows_of(queries):
    return jnp.concatenate([queries[:, h * HD : (h + 1) * HD] for h in range(GROUP)], axis=0)


def stat_rows(peak, total, rows):
    place = lax.broadcasted_iota(jnp.int32, (rows, peak.shape[1]), 0)
    return jnp.where(place == 0, peak, jnp.where(place == 1, total, 0.0))


def packed_stats(peak, total):
    hi = peak.astype(BF).astype(F32)
    rest = peak - hi
    mid = rest.astype(BF).astype(F32)
    low = rest - mid
    total_hi = total.astype(BF).astype(F32)
    total_low = total - total_hi
    place = lax.broadcasted_iota(jnp.int32, (STAT, peak.shape[1]), 0)
    packed = jnp.zeros((STAT, peak.shape[1]), F32)
    for row, part in enumerate((hi, mid, low, total_hi, total_low)):
        packed = jnp.where(place == row, part, packed)
    return packed.astype(BF)


def unpacked_stats(packed):
    rows = packed.astype(F32)
    peak = rows[0:1] + (rows[1:2] + rows[2:3])
    total = rows[3:4] + rows[4:5]
    return peak, total


def store_packed(ref, weighted, peak, total):
    ref[0:HD, :] = weighted.astype(BF)
    ref[HD : HD + STAT, :] = packed_stats(peak, total)


def kv_kernel(x_ref, w_ref, out0, out1, out2, out3, x_buf, w_buf, x_sem, w_sem):
    me = lax.axis_index("sec")
    rows = out0.shape[0]
    parts = w_sem.shape[0]
    depth = w_ref.shape[0] // parts
    flips = (3, 2, 1, 0)
    outs = (out0, out1, out2, out3)

    def x_copy(turn):
        start = pl.multiple_of((me ^ flips[turn]) * rows, rows)
        return pltpu.make_async_copy(
            x_ref.at[pl.ds(start, rows), :],
            x_buf.at[pl.ds(turn * rows, rows), :],
            x_sem.at[turn],
        )

    def w_copy(part):
        span = pl.ds(part * depth, depth)
        return pltpu.make_async_copy(w_ref.at[span, :], w_buf.at[span, :], w_sem.at[part])

    x_copy(0).start()
    for part in range(parts):
        w_copy(part).start()
    for turn in range(1, 4):
        x_copy(turn).start()
    for turn in range(4):
        x_copy(turn).wait()
        mine = x_buf[turn * rows : (turn + 1) * rows, :]
        if turn == 0:
            total = jnp.zeros(out0.shape, F32)
            for part in range(parts):
                w_copy(part).wait()
                span = slice(part * depth, (part + 1) * depth)
                total = total + dot(mine[:, span], w_buf[span, :], ((1,), (0,)))
        else:
            total = dot(mine, w_buf[...], ((1,), (0,)))
        outs[flips[turn]][...] = total.astype(BF)


def cached_kernel(
    owner_ref, slot_ref, len_ref, ctx_ref, q_ref, cache_ref, weighted_ref, stats_ref, live_ref
):
    sec_id, req_id = lax.axis_index("sec"), lax.axis_index("req")
    queries = rows_of(q_ref[...])
    count = cache_ref.shape[1]
    lane = lax.broadcasted_iota(jnp.int32, (count, LANES), 1) % NREQ
    position = lax.broadcasted_iota(jnp.int32, (count, LANES), 0) + sec_id * count
    first = req_id * 2
    live0 = (lane == first) & (position < ctx_ref[0])
    live1 = (lane == first + 1) & (position < ctx_ref[1])
    live = live0 | live1
    scores0 = dot(cache_ref[0, :, 0:HD], queries, ((1,), (1,)))
    scores1 = dot(cache_ref[1, :, 0:HD], queries, ((1,), (1,)))
    scores = jnp.where(live, jnp.where(lane == first, scores0, scores1) * FACTOR, LOW)
    peak = jnp.max(scores, axis=0, keepdims=True)
    weights = jnp.where(live, jnp.exp(scores - peak), 0.0)
    total = jnp.sum(weights, axis=0, keepdims=True)
    weights = weights.astype(BF)
    zero = jnp.zeros_like(weights)
    weighted_ref[...] = dot(
        cache_ref[0, :, HD : 2 * HD], jnp.where(live0, weights, zero), ((0,), (0,))
    ) + dot(cache_ref[1, :, HD : 2 * HD], jnp.where(live1, weights, zero), ((0,), (0,)))
    stats_ref[...] = stat_rows(peak, total, 8)
    blocks = live_ref.shape[0] // BLK
    base = (req_id * lax.axis_size("sec") + sec_id) * blocks
    lane = lax.broadcasted_iota(jnp.int32, (BLK, LANES), 1) % NREQ
    place = lax.broadcasted_iota(jnp.int32, (BLK, LANES), 0)
    for block in range(blocks):
        holder = owner_ref[base + block] * 2 + slot_ref[base + block]
        live_block = (lane == holder) & (place < len_ref[base + block])
        live_ref[block * BLK : (block + 1) * BLK, :] = live_block.astype(F32)


def prompt_kernel(
    q_ref, live_ref, own_ref, a_ref, b_ref, c_ref, cw_ref, cs_ref, kw_ref, ks_ref, send_ref
):
    summed = (own_ref[...].astype(F32) + a_ref[...].astype(F32)) + (
        b_ref[...].astype(F32) + c_ref[...].astype(F32)
    )
    new_kv = summed.astype(BF)
    queries = rows_of(q_ref[...])
    live = live_ref[...] > 0.5
    scores = dot(new_kv[:, 0:HD], queries, ((1,), (1,))) * FACTOR
    scores = jnp.where(live, scores, LOW)
    peak = jnp.max(scores, axis=0, keepdims=True)
    weights = jnp.where(live, jnp.exp(scores - peak), 0.0)
    total = jnp.sum(weights, axis=0, keepdims=True)
    weighted = dot(new_kv[:, HD : 2 * HD], weights.astype(BF), ((0,), (0,)))
    cached_peak, cached_total = cs_ref[0:1, :], cs_ref[1:2, :]
    joint = jnp.maximum(peak, cached_peak)
    scale, cached_scale = jnp.exp(peak - joint), jnp.exp(cached_peak - joint)
    weighted = weighted * scale + cw_ref[...] * cached_scale
    total = total * scale + cached_total * cached_scale
    core = lax.axis_index("req") % 2

    @pl.when(core == 0)
    def _():
        kw_ref[...] = weighted[:, :HALF]
        ks_ref[...] = stat_rows(joint[:, :HALF], total[:, :HALF], 8)
        store_packed(send_ref, weighted[:, HALF:], joint[:, HALF:], total[:, HALF:])

    @pl.when(core == 1)
    def _():
        kw_ref[...] = weighted[:, HALF:]
        ks_ref[...] = stat_rows(joint[:, HALF:], total[:, HALF:], 8)
        store_packed(send_ref, weighted[:, :HALF], joint[:, :HALF], total[:, :HALF])


def joined(w_ref, s_ref, got_refs):
    peaks, totals = [s_ref[0:1, :]], [s_ref[1:2, :]]
    for got_ref in got_refs:
        peak, total = unpacked_stats(got_ref[HD : HD + STAT, :])
        peaks.append(peak)
        totals.append(total)
    joint = peaks[0]
    for peak in peaks[1:]:
        joint = jnp.maximum(joint, peak)
    scales = [jnp.exp(peak - joint) for peak in peaks]
    weighted, total = w_ref[...] * scales[0], totals[0] * scales[0]
    for got_ref, part, scale in zip(got_refs, totals[1:], scales[1:]):
        weighted = weighted + got_ref[0:HD, :].astype(F32) * scale
        total = total + part * scale
    return weighted, joint, total


def join_kernel(w_ref, s_ref, *refs):
    got_refs, (kw_ref, ks_ref, send_ref) = refs[:-3], refs[-3:]
    weighted, peak, total = joined(w_ref, s_ref, got_refs)
    kw_ref[...] = weighted
    ks_ref[...] = stat_rows(peak, total, 8)
    store_packed(send_ref, weighted, peak, total)


def last_kernel(w_ref, s_ref, *refs):
    weighted, _, total = joined(w_ref, s_ref, refs[:-1])
    rows = (weighted / total).T
    for h in range(GROUP // 2):
        refs[-1][:, h * HD : (h + 1) * HD] = rows[h * NREQ : (h + 1) * NREQ, :].astype(BF)


def half_rows(w_ref, core):
    half = w_ref.shape[0] // 2
    return w_ref[pl.ds(pl.multiple_of(core * half, half), half), :]


def first_half_kernel(mine_ref, w_ref, out_ref):
    core = lax.axis_index("req") % 2
    out_ref[...] = dot(mine_ref[...], half_rows(w_ref, core), ((1,), (0,)))


def second_half_kernel(other_ref, w_ref, so_far_ref, out_ref):
    core = lax.axis_index("req") % 2
    more = dot(other_ref[...], half_rows(w_ref, 1 - core), ((1,), (0,)))
    out_ref[...] = (so_far_ref[...] + more).astype(BF)


def shape(dims, dtype):
    return jax.ShapeDtypeStruct(dims, dtype)


def call(kernel, ins, outs, name, flops=0, scratch=()):
    moved = 0
    for _, value in ins:
        moved += value.size * value.dtype.itemsize
    return pl.pallas_call(
        kernel,
        out_shape=outs,
        in_specs=[spec for spec, _ in ins],
        out_specs=jax.tree.map(lambda _: vmem(), outs),
        scratch_shapes=scratch,
        compiler_params=pltpu.CompilerParams(vmem_limit_bytes=32 * 1024 * 1024),
        cost_estimate=pl.CostEstimate(flops=flops, bytes_accessed=moved, transcendentals=0),
        name=name,
    )(*[value for _, value in ins])


STATE = (shape((HD, HALF), F32), shape((8, HALF), F32), shape((HD + STAT, HALF), BF))


def on_device(prompt_x, w_kv, queries, cache, w_out, blk_owner, blk_slot, blk_len, ctx_len):
    sec_count = lax.axis_size("sec")
    req_count = lax.axis_size("req")
    req_id = lax.axis_index("req")
    rows = prompt_x.shape[0] // sec_count
    width = w_kv.shape[1]

    def over(value, sec_flip, req_flip):
        if req_flip == 0:
            return lax.ppermute(value, "sec", [(i, i ^ sec_flip) for i in range(sec_count)])
        if sec_flip == 0:
            return lax.ppermute(value, "req", [(i, i ^ req_flip) for i in range(req_count)])
        pairs = []
        for i in range(sec_count):
            for j in range(req_count):
                pairs.append((i * req_count + j, (i ^ sec_flip) * req_count + (j ^ req_flip)))
        return lax.ppermute(value, ("sec", "req"), pairs)

    tiled = jnp.tile(queries, (NREQ // 2, 1))
    holder = lax.broadcasted_iota(jnp.int32, tiled.shape, 0) // 2
    gathered = jnp.where(holder == req_id, tiled, jnp.zeros_like(tiled))
    for flip in (1, 2, 6):
        gathered = gathered + over(gathered, 0, flip)

    chunk = shape((rows, width), BF)
    chunks = call(
        kv_kernel,
        [(pl.BlockSpec(memory_space=pltpu.HBM), prompt_x), (pl.BlockSpec(memory_space=pltpu.HBM), w_kv)],
        (chunk, chunk, chunk, chunk),
        "new_kv",
        flops=2 * prompt_x.size * width,
        scratch=(
            pltpu.VMEM(prompt_x.shape, BF),
            pltpu.VMEM(w_kv.shape, BF),
            pltpu.SemaphoreType.DMA((4,)),
            pltpu.SemaphoreType.DMA((4,)),
        ),
    )
    arrived = [over(chunks[flip], flip, 0) for flip in (3, 2, 1)]

    cached = call(
        cached_kernel,
        [
            (smem(), blk_owner[:, 0]),
            (smem(), blk_slot),
            (smem(), blk_len),
            (smem(), ctx_len),
            (vmem(), tiled),
            (vmem(), cache[:, :, 0, :]),
        ],
        (shape((HD, LANES), F32), shape((8, LANES), F32), shape((rows, LANES), F32)),
        "cached",
        flops=2 * 4 * cache.shape[1] * HD * LANES,
    )
    kept = call(
        prompt_kernel,
        [
            (vmem(), value)
            for value in (gathered, cached[2], chunks[0], *arrived, cached[0], cached[1])
        ],
        STATE,
        "prompt",
        flops=2 * 2 * rows * HD * LANES,
    )
    kept = call(
        join_kernel,
        [(vmem(), value) for value in (kept[0], kept[1], over(kept[2], 0, 1))],
        STATE,
        "join_core",
    )
    got = [over(kept[2], *flips) for flips in ((1, 2), (1, 0), (0, 2))]
    kept = call(
        join_kernel, [(vmem(), value) for value in (kept[0], kept[1], *got)], STATE, "join_near"
    )
    got = [over(kept[2], *flips) for flips in ((2, 6), (2, 0), (0, 6))]
    mine = call(
        last_kernel,
        [(vmem(), value) for value in (kept[0], kept[1], *got)],
        shape((NREQ, HALF // NREQ * HD), BF),
        "join_far",
    )
    other = over(mine, 0, 1)
    columns = w_out.shape[1]
    flops = w_out.size * NREQ
    so_far = call(
        first_half_kernel,
        [(vmem(), mine), (vmem(), w_out)],
        shape((NREQ, columns), F32),
        "project_mine",
        flops=flops,
    )
    partial_out = call(
        second_half_kernel,
        [(vmem(), other), (vmem(), w_out), (vmem(), so_far)],
        shape((NREQ, columns), BF),
        "project_other",
        flops=flops,
    )
    head_count = lax.axis_size("head")
    pieces = partial_out.reshape(head_count, NREQ // head_count, columns)
    pieces = lax.all_to_all(pieces, "head", 0, 0, tiled=True)
    return jnp.sum(pieces.astype(F32), axis=0).astype(BF)


def solution(mesh):
    return jax.shard_map(
        on_device,
        mesh=mesh,
        in_specs=(
            P("req", "sec"),
            P("sec", "head"),
            P("req", "head"),
            P("req", "sec", "head", None),
            P("head", ("sec", "req")),
            P(),
            P(),
            P(),
            P("req"),
        ),
        out_specs=P("head", ("sec", "req")),
        check_vma=False,
    )
```

```python
import math

import jax
import jax.numpy as jnp
from jax import lax
from jax.experimental import pallas as pl
from jax.experimental.pallas import tpu as pltpu
from jax.sharding import PartitionSpec as P

HD = 128
BLK = 16
GROUP = 16
NREQ = 16
LANES = GROUP * NREQ
HALF = LANES // 2
STAT = 16
LOW = -1e30
FACTOR = 1.0 / math.sqrt(HD)
BF = jnp.bfloat16
F32 = jnp.float32


def vmem():
    return pl.BlockSpec(memory_space=pltpu.VMEM)


def smem():
    return pl.BlockSpec(memory_space=pltpu.SMEM)


def dot(a, b, dims):
    return lax.dot_general(a, b, (dims, ((), ())), preferred_element_type=F32)


def rows_of(queries):
    return jnp.concatenate([queries[:, h * HD : (h + 1) * HD] for h in range(GROUP)], axis=0)


def stat_rows(peak, total, rows):
    place = lax.broadcasted_iota(jnp.int32, (rows, peak.shape[1]), 0)
    return jnp.where(place == 0, peak, jnp.where(place == 1, total, 0.0))


def packed_stats(peak, total):
    hi = peak.astype(BF).astype(F32)
    rest = peak - hi
    mid = rest.astype(BF).astype(F32)
    low = rest - mid
    total_hi = total.astype(BF).astype(F32)
    total_low = total - total_hi
    place = lax.broadcasted_iota(jnp.int32, (STAT, peak.shape[1]), 0)
    packed = jnp.zeros((STAT, peak.shape[1]), F32)
    for row, part in enumerate((hi, mid, low, total_hi, total_low)):
        packed = jnp.where(place == row, part, packed)
    return packed.astype(BF)


def unpacked_stats(packed):
    rows = packed.astype(F32)
    peak = rows[0:1] + (rows[1:2] + rows[2:3])
    total = rows[3:4] + rows[4:5]
    return peak, total


def store_packed(ref, weighted, peak, total):
    ref[0:HD, :] = weighted.astype(BF)
    ref[HD : HD + STAT, :] = packed_stats(peak, total)


def kv_kernel(x_ref, w_ref, out0, out1, out2, out3, x_buf, w_buf, x_sem, w_sem):
    me = lax.axis_index("sec")
    rows = out0.shape[0]
    parts = w_sem.shape[0]
    depth = w_ref.shape[0] // parts
    flips = (3, 2, 1, 0)
    outs = (out0, out1, out2, out3)

    def x_copy(turn):
        start = pl.multiple_of((me ^ flips[turn]) * rows, rows)
        return pltpu.make_async_copy(
            x_ref.at[pl.ds(start, rows), :],
            x_buf.at[pl.ds(turn * rows, rows), :],
            x_sem.at[turn],
        )

    def w_copy(part):
        span = pl.ds(part * depth, depth)
        return pltpu.make_async_copy(w_ref.at[span, :], w_buf.at[span, :], w_sem.at[part])

    x_copy(0).start()
    for part in range(parts):
        w_copy(part).start()
    for turn in range(1, 4):
        x_copy(turn).start()
    for turn in range(4):
        x_copy(turn).wait()
        mine = x_buf[turn * rows : (turn + 1) * rows, :]
        if turn == 0:
            total = jnp.zeros(out0.shape, F32)
            for part in range(parts):
                w_copy(part).wait()
                span = slice(part * depth, (part + 1) * depth)
                total = total + dot(mine[:, span], w_buf[span, :], ((1,), (0,)))
        else:
            total = dot(mine, w_buf[...], ((1,), (0,)))
        outs[flips[turn]][...] = total.astype(BF)


def place_kernel(mine_ref, other_ref, out_ref):
    req_id = lax.axis_index("req")
    place = lax.broadcasted_iota(jnp.int32, (NREQ, 2), 0)
    row = lax.broadcasted_iota(jnp.int32, (NREQ, 2), 1)
    mine = (place == req_id * 2 + row).astype(BF)
    other = (place == (req_id ^ 1) * 2 + row).astype(BF)
    placed = dot(mine, mine_ref[...], ((1,), (0,))) + dot(other, other_ref[...], ((1,), (0,)))
    out_ref[...] = placed.astype(BF)


def cached_kernel(
    owner_ref, slot_ref, len_ref, ctx_ref, q_ref, cache_ref, weighted_ref, stats_ref, live_ref
):
    sec_id, req_id = lax.axis_index("sec"), lax.axis_index("req")
    count = cache_ref.shape[1]
    position = lax.broadcasted_iota(jnp.int32, (GROUP, count), 1) + sec_id * count
    lane = lax.broadcasted_iota(jnp.int32, (GROUP, LANES), 1)
    head = lax.broadcasted_iota(jnp.int32, (GROUP, LANES), 0)
    weighted = jnp.zeros((HD, LANES), F32)
    peaks = jnp.full((1, LANES), LOW, F32)
    totals = jnp.zeros((1, LANES), F32)
    for slot in range(2):
        queries = jnp.concatenate(
            [q_ref[slot : slot + 1, h * HD : (h + 1) * HD] for h in range(GROUP)], axis=0
        )
        live = position < ctx_ref[slot]
        scores = dot(queries, cache_ref[slot, :, 0:HD], ((1,), (1,))) * FACTOR
        scores = jnp.where(live, scores, LOW)
        peak = jnp.max(scores, axis=1, keepdims=True)
        weights = jnp.where(live, jnp.exp(scores - peak), 0.0)
        total = jnp.sum(weights, axis=1, keepdims=True)
        summed = dot(weights.astype(BF), cache_ref[slot, :, HD : 2 * HD], ((1,), (0,)))
        lane_of = lane == head * NREQ + req_id * 2 + slot
        spread = lane_of.astype(BF)
        high = summed.astype(BF)
        low = (summed - high.astype(F32)).astype(BF)
        weighted = weighted + dot(high, spread, ((0,), (0,))) + dot(low, spread, ((0,), (0,)))
        peaks = jnp.maximum(
            peaks, jnp.max(jnp.where(lane_of, peak, LOW), axis=0, keepdims=True)
        )
        totals = totals + jnp.sum(jnp.where(lane_of, total, 0.0), axis=0, keepdims=True)
    weighted_ref[...] = weighted
    stats_ref[...] = stat_rows(peaks, totals, 8)
    blocks = live_ref.shape[0] // BLK
    base = (req_id * lax.axis_size("sec") + sec_id) * blocks
    lane = lax.broadcasted_iota(jnp.int32, (BLK, LANES), 1) % NREQ
    place = lax.broadcasted_iota(jnp.int32, (BLK, LANES), 0)
    for block in range(blocks):
        holder = owner_ref[base + block] * 2 + slot_ref[base + block]
        live_block = (lane == holder) & (place < len_ref[base + block])
        live_ref[block * BLK : (block + 1) * BLK, :] = live_block.astype(F32)


def prompt_kernel(
    q_ref, live_ref, own_ref, a_ref, b_ref, c_ref, cw_ref, cs_ref, kw_ref, ks_ref, send_ref
):
    summed = (own_ref[...].astype(F32) + a_ref[...].astype(F32)) + (
        b_ref[...].astype(F32) + c_ref[...].astype(F32)
    )
    new_kv = summed.astype(BF)
    queries = rows_of(q_ref[...])
    live = live_ref[...] > 0.5
    scores = dot(new_kv[:, 0:HD], queries, ((1,), (1,))) * FACTOR
    scores = jnp.where(live, scores, LOW)
    peak = jnp.max(scores, axis=0, keepdims=True)
    weights = jnp.where(live, jnp.exp(scores - peak), 0.0)
    total = jnp.sum(weights, axis=0, keepdims=True)
    weighted = dot(new_kv[:, HD : 2 * HD], weights.astype(BF), ((0,), (0,)))
    cached_peak, cached_total = cs_ref[0:1, :], cs_ref[1:2, :]
    joint = jnp.maximum(peak, cached_peak)
    scale, cached_scale = jnp.exp(peak - joint), jnp.exp(cached_peak - joint)
    weighted = weighted * scale + cw_ref[...] * cached_scale
    total = total * scale + cached_total * cached_scale
    core = lax.axis_index("req") % 2

    @pl.when(core == 0)
    def _():
        kw_ref[...] = weighted[:, :HALF]
        ks_ref[...] = stat_rows(joint[:, :HALF], total[:, :HALF], 8)
        store_packed(send_ref, weighted[:, HALF:], joint[:, HALF:], total[:, HALF:])

    @pl.when(core == 1)
    def _():
        kw_ref[...] = weighted[:, HALF:]
        ks_ref[...] = stat_rows(joint[:, HALF:], total[:, HALF:], 8)
        store_packed(send_ref, weighted[:, :HALF], joint[:, :HALF], total[:, :HALF])


def joined(w_ref, s_ref, got_refs):
    peaks, totals = [s_ref[0:1, :]], [s_ref[1:2, :]]
    for got_ref in got_refs:
        peak, total = unpacked_stats(got_ref[HD : HD + STAT, :])
        peaks.append(peak)
        totals.append(total)
    joint = peaks[0]
    for peak in peaks[1:]:
        joint = jnp.maximum(joint, peak)
    scales = [jnp.exp(peak - joint) for peak in peaks]
    weighted, total = w_ref[...] * scales[0], totals[0] * scales[0]
    for got_ref, part, scale in zip(got_refs, totals[1:], scales[1:]):
        weighted = weighted + got_ref[0:HD, :].astype(F32) * scale
        total = total + part * scale
    return weighted, joint, total


def join_kernel(w_ref, s_ref, *refs):
    got_refs, (kw_ref, ks_ref, send_ref) = refs[:-3], refs[-3:]
    weighted, peak, total = joined(w_ref, s_ref, got_refs)
    kw_ref[...] = weighted
    ks_ref[...] = stat_rows(peak, total, 8)
    store_packed(send_ref, weighted, peak, total)


def last_kernel(w_ref, s_ref, *refs):
    weighted, _, total = joined(w_ref, s_ref, refs[:-1])
    rows = (weighted / total).T
    for h in range(GROUP // 2):
        refs[-1][:, h * HD : (h + 1) * HD] = rows[h * NREQ : (h + 1) * NREQ, :].astype(BF)


def half_rows(w_ref, core):
    half = w_ref.shape[0] // 2
    return w_ref[pl.ds(pl.multiple_of(core * half, half), half), :]


def first_half_kernel(mine_ref, w_ref, out_ref):
    core = lax.axis_index("req") % 2
    out_ref[...] = dot(mine_ref[...], half_rows(w_ref, core), ((1,), (0,)))


def second_half_kernel(other_ref, w_ref, so_far_ref, out_ref):
    core = lax.axis_index("req") % 2
    more = dot(other_ref[...], half_rows(w_ref, 1 - core), ((1,), (0,)))
    out_ref[...] = (so_far_ref[...] + more).astype(BF)


def shape(dims, dtype):
    return jax.ShapeDtypeStruct(dims, dtype)


def call(kernel, ins, outs, name, flops=0, scratch=(), grant=32):
    moved = 0
    for _, value in ins:
        moved += value.size * value.dtype.itemsize
    return pl.pallas_call(
        kernel,
        out_shape=outs,
        in_specs=[spec for spec, _ in ins],
        out_specs=jax.tree.map(lambda _: vmem(), outs),
        scratch_shapes=scratch,
        compiler_params=pltpu.CompilerParams(vmem_limit_bytes=grant * 1024 * 1024),
        cost_estimate=pl.CostEstimate(flops=flops, bytes_accessed=moved, transcendentals=0),
        name=name,
    )(*[value for _, value in ins])


STATE = (shape((HD, HALF), F32), shape((8, HALF), F32), shape((HD + STAT, HALF), BF))


def on_device(prompt_x, w_kv, queries, cache, w_out, blk_owner, blk_slot, blk_len, ctx_len):
    sec_count = lax.axis_size("sec")
    req_count = lax.axis_size("req")
    req_id = lax.axis_index("req")
    rows = prompt_x.shape[0] // sec_count
    width = w_kv.shape[1]

    def over(value, sec_flip, req_flip):
        if req_flip == 0:
            return lax.ppermute(value, "sec", [(i, i ^ sec_flip) for i in range(sec_count)])
        if sec_flip == 0:
            return lax.ppermute(value, "req", [(i, i ^ req_flip) for i in range(req_count)])
        pairs = []
        for i in range(sec_count):
            for j in range(req_count):
                pairs.append((i * req_count + j, (i ^ sec_flip) * req_count + (j ^ req_flip)))
        return lax.ppermute(value, ("sec", "req"), pairs)

    chunk = shape((rows, width), BF)
    hbm = pl.BlockSpec(memory_space=pltpu.HBM)
    other_queries = over(queries, 0, 1)
    chunks = call(
        kv_kernel,
        [(hbm, prompt_x), (hbm, w_kv)],
        (chunk, chunk, chunk, chunk),
        "new_kv",
        flops=2 * prompt_x.size * width,
        scratch=(
            pltpu.VMEM(prompt_x.shape, BF),
            pltpu.VMEM(w_kv.shape, BF),
            pltpu.SemaphoreType.DMA((4,)),
            pltpu.SemaphoreType.DMA((4,)),
        ),
        grant=52,
    )
    chunks, other_queries = lax.optimization_barrier((chunks, other_queries))

    gathered = call(
        place_kernel,
        [(vmem(), queries), (vmem(), other_queries)],
        shape((NREQ, queries.shape[1]), BF),
        "place",
    )
    for flip in (2, 6):
        gathered = gathered + over(gathered, 0, flip)
    arrived = [over(chunks[flip], flip, 0) for flip in (3, 2, 1)]

    cached = call(
        cached_kernel,
        [
            (smem(), blk_owner[:, 0]),
            (smem(), blk_slot),
            (smem(), blk_len),
            (smem(), ctx_len),
            (vmem(), queries),
            (vmem(), cache[:, :, 0, :]),
        ],
        (shape((HD, LANES), F32), shape((8, LANES), F32), shape((rows, LANES), F32)),
        "cached",
        flops=2 * 4 * cache.shape[1] * HD * LANES,
    )
    kept = call(
        prompt_kernel,
        [
            (vmem(), value)
            for value in (gathered, cached[2], chunks[0], *arrived, cached[0], cached[1])
        ],
        STATE,
        "prompt",
        flops=2 * 2 * rows * HD * LANES,
    )
    kept = call(
        join_kernel,
        [(vmem(), value) for value in (kept[0], kept[1], over(kept[2], 0, 1))],
        STATE,
        "join_core",
    )
    got = [over(kept[2], *flips) for flips in ((1, 2), (1, 0), (0, 2))]
    kept = call(
        join_kernel, [(vmem(), value) for value in (kept[0], kept[1], *got)], STATE, "join_near"
    )
    got = [over(kept[2], *flips) for flips in ((2, 6), (2, 0), (0, 6))]
    mine = call(
        last_kernel,
        [(vmem(), value) for value in (kept[0], kept[1], *got)],
        shape((NREQ, HALF // NREQ * HD), BF),
        "join_far",
    )
    other = over(mine, 0, 1)
    columns = w_out.shape[1]
    flops = w_out.size * NREQ
    so_far = call(
        first_half_kernel,
        [(vmem(), mine), (vmem(), w_out)],
        shape((NREQ, columns), F32),
        "project_mine",
        flops=flops,
    )
    partial_out = call(
        second_half_kernel,
        [(vmem(), other), (vmem(), w_out), (vmem(), so_far)],
        shape((NREQ, columns), BF),
        "project_other",
        flops=flops,
    )
    head_count = lax.axis_size("head")
    pieces = partial_out.reshape(head_count, NREQ // head_count, columns)
    pieces = lax.all_to_all(pieces, "head", 0, 0, tiled=True)
    return jnp.sum(pieces.astype(F32), axis=0).astype(BF)


def solution(mesh):
    return jax.shard_map(
        on_device,
        mesh=mesh,
        in_specs=(
            P("req", "sec"),
            P("sec", "head"),
            P("req", "head"),
            P("req", "sec", "head", None),
            P("head", ("sec", "req")),
            P(),
            P(),
            P(),
            P("req"),
        ),
        out_specs=P("head", ("sec", "req")),
        check_vma=False,
    )
```

```python
import math

import jax
import jax.numpy as jnp
from jax import lax
from jax.experimental import pallas as pl
from jax.experimental.pallas import tpu as pltpu
from jax.sharding import PartitionSpec as P

HD = 128
BLK = 16
GROUP = 16
NREQ = 16
LANES = GROUP * NREQ
STAT = 16
LOW = -1e30
FACTOR = 1.0 / math.sqrt(HD)
BF = jnp.bfloat16
F32 = jnp.float32


def vmem():
    return pl.BlockSpec(memory_space=pltpu.VMEM)


def smem():
    return pl.BlockSpec(memory_space=pltpu.SMEM)


def dot(a, b, dims):
    return lax.dot_general(a, b, (dims, ((), ())), preferred_element_type=F32)


def rows_of(queries):
    return jnp.concatenate([queries[:, h * HD : (h + 1) * HD] for h in range(GROUP)], axis=0)


def stat_rows(peak, total, rows):
    place = lax.broadcasted_iota(jnp.int32, (rows, peak.shape[1]), 0)
    return jnp.where(place == 0, peak, jnp.where(place == 1, total, 0.0))


def packed_stats(peak, total):
    hi = peak.astype(BF).astype(F32)
    rest = peak - hi
    mid = rest.astype(BF).astype(F32)
    low = rest - mid
    total_hi = total.astype(BF).astype(F32)
    total_low = total - total_hi
    place = lax.broadcasted_iota(jnp.int32, (STAT, peak.shape[1]), 0)
    packed = jnp.zeros((STAT, peak.shape[1]), F32)
    for row, part in enumerate((hi, mid, low, total_hi, total_low)):
        packed = jnp.where(place == row, part, packed)
    return packed.astype(BF)


def unpacked_stats(packed):
    rows = packed.astype(F32)
    peak = rows[0:1] + (rows[1:2] + rows[2:3])
    total = rows[3:4] + rows[4:5]
    return peak, total


def store_packed(ref, weighted, peak, total):
    ref[0:HD, :] = weighted.astype(BF)
    ref[HD : HD + STAT, :] = packed_stats(peak, total)


def kv_kernel(x_ref, w_ref, out0, out1, out2, out3, x_buf, w_buf, sems):
    sec_id = lax.axis_index("sec")
    rows = out0.shape[0]
    copies = (
        pltpu.make_async_copy(w_ref, w_buf, sems.at[0]),
        pltpu.make_async_copy(x_ref, x_buf, sems.at[1]),
    )
    for copy in copies:
        copy.start()
    for copy in copies:
        copy.wait()
    for flip, out in enumerate((out0, out1, out2, out3)):
        start = pl.multiple_of((sec_id ^ flip) * rows, rows)
        out[...] = dot(x_buf[pl.ds(start, rows), :], w_buf[...], ((1,), (0,))).astype(BF)


def sum_kernel(own_ref, a_ref, b_ref, c_ref, out_ref):
    summed = (own_ref[...].astype(F32) + a_ref[...].astype(F32)) + (
        b_ref[...].astype(F32) + c_ref[...].astype(F32)
    )
    out_ref[...] = summed.astype(BF)


def cached_kernel(
    owner_ref, slot_ref, len_ref, ctx_ref, q_ref, cache_ref, weighted_ref, stats_ref, live_ref
):
    sec_id, req_id = lax.axis_index("sec"), lax.axis_index("req")
    count = cache_ref.shape[1]
    position = lax.broadcasted_iota(jnp.int32, (GROUP, count), 1) + sec_id * count
    lane = lax.broadcasted_iota(jnp.int32, (GROUP, LANES), 1)
    head = lax.broadcasted_iota(jnp.int32, (GROUP, LANES), 0)
    weighted = jnp.zeros((HD, LANES), F32)
    peaks = jnp.full((1, LANES), LOW, F32)
    totals = jnp.zeros((1, LANES), F32)
    for slot in range(2):
        queries = jnp.concatenate(
            [q_ref[slot : slot + 1, h * HD : (h + 1) * HD] for h in range(GROUP)], axis=0
        )
        live = position < ctx_ref[slot]
        scores = dot(queries, cache_ref[slot, :, 0:HD], ((1,), (1,))) * FACTOR
        scores = jnp.where(live, scores, LOW)
        peak = jnp.max(scores, axis=1, keepdims=True)
        weights = jnp.where(live, jnp.exp(scores - peak), 0.0)
        total = jnp.sum(weights, axis=1, keepdims=True)
        summed = dot(weights.astype(BF), cache_ref[slot, :, HD : 2 * HD], ((1,), (0,)))
        lane_of = lane == head * NREQ + req_id * 2 + slot
        spread = lane_of.astype(BF)
        high = summed.astype(BF)
        low = (summed - high.astype(F32)).astype(BF)
        weighted = weighted + dot(high, spread, ((0,), (0,))) + dot(low, spread, ((0,), (0,)))
        peaks = jnp.maximum(
            peaks, jnp.max(jnp.where(lane_of, peak, LOW), axis=0, keepdims=True)
        )
        totals = totals + jnp.sum(jnp.where(lane_of, total, 0.0), axis=0, keepdims=True)
    weighted_ref[...] = weighted
    stats_ref[...] = stat_rows(peaks, totals, 8)
    blocks = live_ref.shape[0] // BLK
    base = (req_id * lax.axis_size("sec") + sec_id) * blocks
    lane = lax.broadcasted_iota(jnp.int32, (BLK, LANES), 1) % NREQ
    place = lax.broadcasted_iota(jnp.int32, (BLK, LANES), 0)
    for block in range(blocks):
        holder = owner_ref[base + block] * 2 + slot_ref[base + block]
        live_block = (lane == holder) & (place < len_ref[base + block])
        live_ref[block * BLK : (block + 1) * BLK, :] = live_block.astype(F32)


def place_kernel(mine_ref, other_ref, out_ref):
    req_id = lax.axis_index("req")
    place = lax.broadcasted_iota(jnp.int32, (NREQ, 2), 0)
    row = lax.broadcasted_iota(jnp.int32, (NREQ, 2), 1)
    mine = (place == req_id * 2 + row).astype(BF)
    other = (place == (req_id ^ 1) * 2 + row).astype(BF)
    placed = dot(mine, mine_ref[...], ((1,), (0,))) + dot(other, other_ref[...], ((1,), (0,)))
    out_ref[...] = placed.astype(BF)


def prompt_kernel(q_ref, live_ref, kv_ref, cw_ref, cs_ref, kw_ref, ks_ref, send_ref):
    new_kv = kv_ref[...]
    queries = rows_of(q_ref[...])
    live = live_ref[...] > 0.5
    scores = dot(new_kv[:, 0:HD], queries, ((1,), (1,))) * FACTOR
    scores = jnp.where(live, scores, LOW)
    peak = jnp.max(scores, axis=0, keepdims=True)
    weights = jnp.where(live, jnp.exp(scores - peak), 0.0)
    total = jnp.sum(weights, axis=0, keepdims=True)
    weighted = dot(new_kv[:, HD : 2 * HD], weights.astype(BF), ((0,), (0,)))
    cached_peak, cached_total = cs_ref[0:1, :], cs_ref[1:2, :]
    joint = jnp.maximum(peak, cached_peak)
    scale, cached_scale = jnp.exp(peak - joint), jnp.exp(cached_peak - joint)
    weighted = weighted * scale + cw_ref[...] * cached_scale
    total = total * scale + cached_total * cached_scale
    kw_ref[...] = weighted
    ks_ref[...] = stat_rows(joint, total, 8)
    store_packed(send_ref, weighted, joint, total)


def joined(w_ref, s_ref, got_refs):
    peaks, totals = [s_ref[0:1, :]], [s_ref[1:2, :]]
    for got_ref in got_refs:
        peak, total = unpacked_stats(got_ref[HD : HD + STAT, :])
        peaks.append(peak)
        totals.append(total)
    joint = peaks[0]
    for peak in peaks[1:]:
        joint = jnp.maximum(joint, peak)
    scales = [jnp.exp(peak - joint) for peak in peaks]
    weighted, total = w_ref[...] * scales[0], totals[0] * scales[0]
    for got_ref, part, scale in zip(got_refs, totals[1:], scales[1:]):
        weighted = weighted + got_ref[0:HD, :].astype(F32) * scale
        total = total + part * scale
    return weighted, joint, total


def join_kernel(w_ref, s_ref, *refs):
    got_refs, (kw_ref, ks_ref, send_ref) = refs[:-3], refs[-3:]
    weighted, peak, total = joined(w_ref, s_ref, got_refs)
    kw_ref[...] = weighted
    ks_ref[...] = stat_rows(peak, total, 8)
    store_packed(send_ref, weighted, peak, total)


def project_kernel(w_ref, s_ref, out_w_ref, *refs):
    weighted, _, total = joined(w_ref, s_ref, refs[:-1])
    rows = (weighted / total).T.astype(BF)
    attended = jnp.concatenate(
        [rows[h * NREQ : (h + 1) * NREQ, :] for h in range(GROUP)], axis=1
    )
    refs[-1][...] = dot(attended, out_w_ref[...], ((1,), (0,))).astype(BF)


def shape(dims, dtype):
    return jax.ShapeDtypeStruct(dims, dtype)


def call(kernel, ins, outs, name, flops=0, scratch=(), grant=32):
    moved = 0
    for _, value in ins:
        moved += value.size * value.dtype.itemsize
    return pl.pallas_call(
        kernel,
        out_shape=outs,
        in_specs=[spec for spec, _ in ins],
        out_specs=jax.tree.map(lambda _: vmem(), outs),
        scratch_shapes=scratch,
        compiler_params=pltpu.CompilerParams(vmem_limit_bytes=grant * 1024 * 1024),
        cost_estimate=pl.CostEstimate(flops=flops, bytes_accessed=moved, transcendentals=0),
        name=name,
    )(*[value for _, value in ins])


STATE = (shape((HD, LANES), F32), shape((8, LANES), F32), shape((HD + STAT, LANES), BF))


def on_device(prompt_x, w_kv, queries, cache, w_out, blk_owner, blk_slot, blk_len, ctx_len):
    sec_count = lax.axis_size("sec")
    req_count = lax.axis_size("req")
    req_id = lax.axis_index("req")
    rows = prompt_x.shape[0] // sec_count
    width = w_kv.shape[1]

    def over(value, sec_flip, req_flip):
        if req_flip == 0:
            return lax.ppermute(value, "sec", [(i, i ^ sec_flip) for i in range(sec_count)])
        if sec_flip == 0:
            return lax.ppermute(value, "req", [(i, i ^ req_flip) for i in range(req_count)])
        pairs = []
        for i in range(sec_count):
            for j in range(req_count):
                pairs.append((i * req_count + j, (i ^ sec_flip) * req_count + (j ^ req_flip)))
        return lax.ppermute(value, ("sec", "req"), pairs)

    chunk = shape((rows, width), BF)
    hbm = pl.BlockSpec(memory_space=pltpu.HBM)
    other_queries = over(queries, 0, 1)
    chunks = call(
        kv_kernel,
        [(hbm, prompt_x), (hbm, w_kv)],
        (chunk, chunk, chunk, chunk),
        "new_kv",
        flops=2 * prompt_x.size * width,
        scratch=(
            pltpu.VMEM(prompt_x.shape, BF),
            pltpu.VMEM(w_kv.shape, BF),
            pltpu.SemaphoreType.DMA((2,)),
        ),
        grant=52,
    )
    chunks, other_queries = lax.optimization_barrier((chunks, other_queries))

    gathered = call(
        place_kernel,
        [(vmem(), queries), (vmem(), other_queries)],
        shape((NREQ, queries.shape[1]), BF),
        "place",
    )
    gathered = gathered + over(gathered, 0, 2)
    arrived = [over(chunks[flip], flip, 0) for flip in (3, 2, 1)]
    gathered = gathered + over(gathered, 0, 6)
    cached_weighted, cached_stats, live = call(
        cached_kernel,
        [
            (smem(), blk_owner[:, 0]),
            (smem(), blk_slot),
            (smem(), blk_len),
            (smem(), ctx_len),
            (vmem(), queries),
            (vmem(), cache[:, :, 0, :]),
        ],
        (shape((HD, LANES), F32), shape((8, LANES), F32), shape((rows, LANES), F32)),
        "cached",
        flops=2 * 4 * cache.shape[1] * HD * LANES,
    )
    new_kv = call(
        sum_kernel, [(vmem(), value) for value in (chunks[0], *arrived)], chunk, "kv_sum"
    )
    kept = call(
        prompt_kernel,
        [
            (vmem(), value) for value in (gathered, live, new_kv, cached_weighted, cached_stats)
        ],
        STATE,
        "prompt",
        flops=2 * 2 * rows * HD * LANES,
    )
    for name, moves in (
        ("join_core", ((0, 1),)),
        ("join_near", ((1, 2), (1, 0), (0, 2))),
    ):
        got = [over(kept[2], *flips) for flips in moves]
        kept = call(
            join_kernel, [(vmem(), value) for value in (kept[0], kept[1], *got)], STATE, name
        )
    got = [over(kept[2], *flips) for flips in ((2, 6), (2, 0), (0, 6))]
    columns = w_out.shape[1]
    partial_out = call(
        project_kernel,
        [(vmem(), value) for value in (kept[0], kept[1], w_out, *got)],
        shape((NREQ, columns), BF),
        "join_far_project",
        flops=2 * w_out.size * NREQ,
    )
    head_count = lax.axis_size("head")
    pieces = partial_out.reshape(head_count, NREQ // head_count, columns)
    pieces = lax.all_to_all(pieces, "head", 0, 0, tiled=True)
    return jnp.sum(pieces.astype(F32), axis=0).astype(BF)


def solution(mesh):
    return jax.shard_map(
        on_device,
        mesh=mesh,
        in_specs=(
            P("req", "sec"),
            P("sec", "head"),
            P("req", "head"),
            P("req", "sec", "head", None),
            P("head", ("sec", "req")),
            P(),
            P(),
            P(),
            P("req"),
        ),
        out_specs=P("head", ("sec", "req")),
        check_vma=False,
    )
```

```python
import math

import jax
import jax.numpy as jnp
from jax import lax
from jax.experimental import pallas as pl
from jax.experimental.pallas import tpu as pltpu
from jax.sharding import PartitionSpec as P

HD = 128
BLK = 16
GROUP = 16
NREQ = 16
LANES = GROUP * NREQ
STAT = 16
LOW = -1e30
FACTOR = 1.0 / math.sqrt(HD)
BF = jnp.bfloat16
F32 = jnp.float32


def vmem():
    return pl.BlockSpec(memory_space=pltpu.VMEM)


def dot(a, b, dims):
    return lax.dot_general(a, b, (dims, ((), ())), preferred_element_type=F32)


def rows_of(queries):
    return jnp.concatenate([queries[:, h * HD : (h + 1) * HD] for h in range(GROUP)], axis=0)


def stat_rows(peak, total, rows):
    place = lax.broadcasted_iota(jnp.int32, (rows, peak.shape[1]), 0)
    return jnp.where(place == 0, peak, jnp.where(place == 1, total, 0.0))


def packed_stats(peak, total):
    hi = peak.astype(BF).astype(F32)
    rest = peak - hi
    mid = rest.astype(BF).astype(F32)
    low = rest - mid
    total_hi = total.astype(BF).astype(F32)
    total_low = total - total_hi
    place = lax.broadcasted_iota(jnp.int32, (STAT, peak.shape[1]), 0)
    packed = jnp.zeros((STAT, peak.shape[1]), F32)
    for row, part in enumerate((hi, mid, low, total_hi, total_low)):
        packed = jnp.where(place == row, part, packed)
    return packed.astype(BF)


def unpacked_stats(packed):
    rows = packed.astype(F32)
    peak = rows[0:1] + (rows[1:2] + rows[2:3])
    total = rows[3:4] + rows[4:5]
    return peak, total


def store_packed(ref, weighted, peak, total):
    ref[0:HD, :] = weighted.astype(BF)
    ref[HD : HD + STAT, :] = packed_stats(peak, total)


def kv_kernel(x_ref, w_ref, out0, out1, out2, out3, x_buf, w_buf, sems):
    sec_id = lax.axis_index("sec")
    rows = out0.shape[0]
    copies = (
        pltpu.make_async_copy(w_ref, w_buf, sems.at[0]),
        pltpu.make_async_copy(x_ref, x_buf, sems.at[1]),
    )
    for copy in copies:
        copy.start()
    for copy in copies:
        copy.wait()
    for flip, out in enumerate((out0, out1, out2, out3)):
        start = pl.multiple_of((sec_id ^ flip) * rows, rows)
        out[...] = dot(x_buf[pl.ds(start, rows), :], w_buf[...], ((1,), (0,))).astype(BF)


def sum_kernel(own_ref, a_ref, b_ref, c_ref, out_ref):
    summed = (own_ref[...].astype(F32) + a_ref[...].astype(F32)) + (
        b_ref[...].astype(F32) + c_ref[...].astype(F32)
    )
    out_ref[...] = summed.astype(BF)


def cached_kernel(
    owner_ref, slot_ref, len_ref, ctx_ref, q_ref, cache_ref, weighted_ref, stats_ref, live_ref
):
    sec_id, req_id = lax.axis_index("sec"), lax.axis_index("req")
    count = cache_ref.shape[1]
    position = lax.broadcasted_iota(jnp.int32, (GROUP, count), 1) + sec_id * count
    lane = lax.broadcasted_iota(jnp.int32, (GROUP, LANES), 1)
    head = lax.broadcasted_iota(jnp.int32, (GROUP, LANES), 0)
    weighted = jnp.zeros((HD, LANES), F32)
    peaks = jnp.full((1, LANES), LOW, F32)
    totals = jnp.zeros((1, LANES), F32)
    for slot in range(2):
        queries = jnp.concatenate(
            [q_ref[slot : slot + 1, h * HD : (h + 1) * HD] for h in range(GROUP)], axis=0
        )
        live = position < ctx_ref[0:1, slot : slot + 1]
        scores = dot(queries, cache_ref[slot, :, 0:HD], ((1,), (1,))) * FACTOR
        scores = jnp.where(live, scores, LOW)
        peak = jnp.max(scores, axis=1, keepdims=True)
        weights = jnp.where(live, jnp.exp(scores - peak), 0.0)
        total = jnp.sum(weights, axis=1, keepdims=True)
        summed = dot(weights.astype(BF), cache_ref[slot, :, HD : 2 * HD], ((1,), (0,)))
        lane_of = lane == head * NREQ + req_id * 2 + slot
        spread = lane_of.astype(BF)
        high = summed.astype(BF)
        low = (summed - high.astype(F32)).astype(BF)
        weighted = weighted + dot(high, spread, ((0,), (0,))) + dot(low, spread, ((0,), (0,)))
        peaks = jnp.maximum(
            peaks, jnp.max(jnp.where(lane_of, peak, LOW), axis=0, keepdims=True)
        )
        totals = totals + jnp.sum(jnp.where(lane_of, total, 0.0), axis=0, keepdims=True)
    weighted_ref[...] = weighted
    stats_ref[...] = stat_rows(peaks, totals, 8)

    rows, blocks = live_ref.shape[0], owner_ref.shape[1]
    first = (req_id * lax.axis_size("sec") + sec_id) * (rows // BLK)
    token = lax.broadcasted_iota(jnp.int32, (rows, blocks), 0)
    block = lax.broadcasted_iota(jnp.int32, (rows, blocks), 1)
    mine = block == token // BLK + first
    holder = owner_ref[...] * 2 + slot_ref[...]
    holder = jnp.sum(jnp.where(mine, holder, 0).astype(F32), axis=1, keepdims=True)
    length = jnp.sum(jnp.where(mine, len_ref[...], 0).astype(F32), axis=1, keepdims=True)
    lane = lax.broadcasted_iota(jnp.int32, (rows, LANES), 1) % NREQ
    place = lax.broadcasted_iota(jnp.int32, (rows, LANES), 0) % BLK
    live = (lane.astype(F32) == holder) & (place.astype(F32) < length)
    live_ref[...] = live.astype(F32)


def pair_up(mine, other, mine_is_first):
    rows = mine.shape[0]
    place = lax.broadcasted_iota(jnp.int32, (2 * rows, rows), 0)
    row = lax.broadcasted_iota(jnp.int32, (2 * rows, rows), 1)
    lower, upper = (place == row).astype(F32), (place == row + rows).astype(F32)
    first = mine_is_first.astype(F32)
    mine_place = (lower * first + upper * (1.0 - first)).astype(BF)
    other_place = (upper * first + lower * (1.0 - first)).astype(BF)
    both = dot(mine_place, mine, ((1,), (0,))) + dot(other_place, other, ((1,), (0,)))
    return both.astype(BF)


def core_pair_kernel(mine_ref, other_ref, out_ref):
    req_id = lax.axis_index("req")
    out_ref[...] = pair_up(mine_ref[...], other_ref[...], req_id % 2 == 0)


def y_pair_kernel(mine_ref, other_ref, out_ref):
    req_id = lax.axis_index("req")
    out_ref[...] = pair_up(mine_ref[...], other_ref[...], req_id // 2 % 2 == 0)


def prompt_kernel(
    mine_ref, other_ref, live_ref, kv_ref, cw_ref, cs_ref, kw_ref, ks_ref, send_ref
):
    new_kv = kv_ref[...]
    req_id = lax.axis_index("req")
    queries = rows_of(pair_up(mine_ref[...], other_ref[...], req_id < lax.axis_size("req") // 2))
    live = live_ref[...] > 0.5
    scores = dot(new_kv[:, 0:HD], queries, ((1,), (1,))) * FACTOR
    scores = jnp.where(live, scores, LOW)
    peak = jnp.max(scores, axis=0, keepdims=True)
    weights = jnp.where(live, jnp.exp(scores - peak), 0.0)
    total = jnp.sum(weights, axis=0, keepdims=True)
    weighted = dot(new_kv[:, HD : 2 * HD], weights.astype(BF), ((0,), (0,)))
    cached_peak, cached_total = cs_ref[0:1, :], cs_ref[1:2, :]
    joint = jnp.maximum(peak, cached_peak)
    scale, cached_scale = jnp.exp(peak - joint), jnp.exp(cached_peak - joint)
    weighted = weighted * scale + cw_ref[...] * cached_scale
    total = total * scale + cached_total * cached_scale
    kw_ref[...] = weighted
    ks_ref[...] = stat_rows(joint, total, 8)
    store_packed(send_ref, weighted, joint, total)


def joined(w_ref, s_ref, got_refs):
    peaks, totals = [s_ref[0:1, :]], [s_ref[1:2, :]]
    for got_ref in got_refs:
        peak, total = unpacked_stats(got_ref[HD : HD + STAT, :])
        peaks.append(peak)
        totals.append(total)
    joint = peaks[0]
    for peak in peaks[1:]:
        joint = jnp.maximum(joint, peak)
    scales = [jnp.exp(peak - joint) for peak in peaks]
    weighted, total = w_ref[...] * scales[0], totals[0] * scales[0]
    for got_ref, part, scale in zip(got_refs, totals[1:], scales[1:]):
        weighted = weighted + got_ref[0:HD, :].astype(F32) * scale
        total = total + part * scale
    return weighted, joint, total


def join_kernel(w_ref, s_ref, *refs):
    got_refs, (kw_ref, ks_ref, send_ref) = refs[:-3], refs[-3:]
    weighted, peak, total = joined(w_ref, s_ref, got_refs)
    kw_ref[...] = weighted
    ks_ref[...] = stat_rows(peak, total, 8)
    store_packed(send_ref, weighted, peak, total)


def far_kernel(first_ref, second_ref, kw_ref, ks_ref, send_ref):
    use_second = (lax.axis_index("req") % 2).astype(F32)
    peak, total = unpacked_stats(first_ref[HD : HD + STAT, :])
    peak_2, total_2 = unpacked_stats(second_ref[HD : HD + STAT, :])
    joint = jnp.maximum(peak, peak_2)
    scale, scale_2 = jnp.exp(peak - joint), jnp.exp(peak_2 - joint) * use_second
    weighted = first_ref[0:HD, :].astype(F32) * scale + second_ref[0:HD, :].astype(F32) * scale_2
    total = total * scale + total_2 * scale_2
    kw_ref[...] = weighted
    ks_ref[...] = stat_rows(joint, total, 8)
    store_packed(send_ref, weighted, joint, total)


def project_kernel(w_ref, s_ref, far_w_ref, far_s_ref, out_w_ref, got_ref, out_ref):
    weighted, peak, total = joined(w_ref, s_ref, (got_ref,))
    far_peak, far_total = far_s_ref[0:1, :], far_s_ref[1:2, :]
    joint = jnp.maximum(peak, far_peak)
    scale, far_scale = jnp.exp(peak - joint), jnp.exp(far_peak - joint)
    weighted = weighted * scale + far_w_ref[...] * far_scale
    total = total * scale + far_total * far_scale
    rows = (weighted / total).T.astype(BF)
    attended = jnp.concatenate(
        [rows[h * NREQ : (h + 1) * NREQ, :] for h in range(GROUP)], axis=1
    )
    out_ref[...] = dot(attended, out_w_ref[...], ((1,), (0,))).astype(BF)


def shape(dims, dtype):
    return jax.ShapeDtypeStruct(dims, dtype)


def call(kernel, ins, outs, name, flops=0, scratch=(), grant=32):
    moved = 0
    for _, value in ins:
        moved += value.size * value.dtype.itemsize
    return pl.pallas_call(
        kernel,
        out_shape=outs,
        in_specs=[spec for spec, _ in ins],
        out_specs=jax.tree.map(lambda _: vmem(), outs),
        scratch_shapes=scratch,
        compiler_params=pltpu.CompilerParams(vmem_limit_bytes=grant * 1024 * 1024),
        cost_estimate=pl.CostEstimate(flops=flops, bytes_accessed=moved, transcendentals=0),
        name=name,
    )(*[value for _, value in ins])


STATE = (shape((HD, LANES), F32), shape((8, LANES), F32), shape((HD + STAT, LANES), BF))


def on_device(prompt_x, w_kv, queries, cache, w_out, blk_owner, blk_slot, blk_len, ctx_len):
    sec_count = lax.axis_size("sec")
    req_count = lax.axis_size("req")
    req_id = lax.axis_index("req")
    rows = prompt_x.shape[0] // sec_count
    width = w_kv.shape[1]

    def over(value, sec_flip, req_flip):
        if req_flip == 0:
            return lax.ppermute(value, "sec", [(i, i ^ sec_flip) for i in range(sec_count)])
        if sec_flip == 0:
            return lax.ppermute(value, "req", [(i, i ^ req_flip) for i in range(req_count)])
        return over_cores(value, (sec_flip, req_flip), (sec_flip, req_flip))

    def over_cores(value, flips_0, flips_1):
        pairs = []
        for i in range(sec_count):
            for j in range(req_count):
                sec_flip, req_flip = flips_1 if j % 2 else flips_0
                pairs.append((i * req_count + j, (i ^ sec_flip) * req_count + (j ^ req_flip)))
        return lax.ppermute(value, ("sec", "req"), pairs)

    chunk = shape((rows, width), BF)
    hbm = pl.BlockSpec(memory_space=pltpu.HBM)
    other_queries = over(queries, 0, 1)
    chunks = call(
        kv_kernel,
        [(hbm, prompt_x), (hbm, w_kv)],
        (chunk, chunk, chunk, chunk),
        "new_kv",
        flops=2 * prompt_x.size * width,
        scratch=(
            pltpu.VMEM(prompt_x.shape, BF),
            pltpu.VMEM(w_kv.shape, BF),
            pltpu.SemaphoreType.DMA((2,)),
        ),
        grant=52,
    )
    chunks, other_queries = lax.optimization_barrier((chunks, other_queries))

    def paired(kernel, mine, other, name):
        return call(
            kernel,
            [(vmem(), mine), (vmem(), other)],
            shape((2 * mine.shape[0], mine.shape[1]), BF),
            name,
        )

    of_chip = paired(core_pair_kernel, queries, other_queries, "core_pair")
    arrived = [over(chunks[flip], flip, 0) for flip in (3, 2, 1)]
    of_half = paired(y_pair_kernel, of_chip, over(of_chip, 0, 2), "y_pair")
    of_other_half = over(of_half, 0, 6)
    cached_weighted, cached_stats, live = call(
        cached_kernel,
        [
            (vmem(), blk_owner.reshape(1, -1)),
            (vmem(), blk_slot.reshape(1, -1)),
            (vmem(), blk_len.reshape(1, -1)),
            (vmem(), ctx_len.reshape(1, -1)),
            (vmem(), queries),
            (vmem(), cache[:, :, 0, :]),
        ],
        (shape((HD, LANES), F32), shape((8, LANES), F32), shape((rows, LANES), F32)),
        "cached",
        flops=2 * 4 * cache.shape[1] * HD * LANES,
    )
    new_kv = call(
        sum_kernel, [(vmem(), value) for value in (chunks[0], *arrived)], chunk, "kv_sum"
    )
    kept = call(
        prompt_kernel,
        [
            (vmem(), value)
            for value in (of_half, of_other_half, live, new_kv, cached_weighted, cached_stats)
        ],
        STATE,
        "prompt",
        flops=2 * 2 * rows * HD * LANES,
    )
    for name, moves in (
        ("join_core", ((0, 1),)),
        ("join_near", ((1, 2), (1, 0), (0, 2))),
    ):
        got = [over(kept[2], *flips) for flips in moves]
        kept = call(
            join_kernel, [(vmem(), value) for value in (kept[0], kept[1], *got)], STATE, name
        )
    got = [
        over_cores(kept[2], (0, 6), flips) for flips in ((2, 0), (2, 6))
    ]
    far = call(far_kernel, [(vmem(), value) for value in got], STATE, "join_far")
    columns = w_out.shape[1]
    partial_out = call(
        project_kernel,
        [
            (vmem(), value)
            for value in (kept[0], kept[1], far[0], far[1], w_out, over(far[2], 0, 1))
        ],
        shape((NREQ, columns), BF),
        "project",
        flops=2 * w_out.size * NREQ,
    )
    head_count = lax.axis_size("head")
    pieces = partial_out.reshape(head_count, NREQ // head_count, columns)
    pieces = lax.all_to_all(pieces, "head", 0, 0, tiled=True)
    return jnp.sum(pieces.astype(F32), axis=0).astype(BF)


def solution(mesh):
    return jax.shard_map(
        on_device,
        mesh=mesh,
        in_specs=(
            P("req", "sec"),
            P("sec", "head"),
            P("req", "head"),
            P("req", "sec", "head", None),
            P("head", ("sec", "req")),
            P(),
            P(),
            P(),
            P("req"),
        ),
        out_specs=P("head", ("sec", "req")),
        check_vma=False,
    )
```

```python
import math

import jax
import jax.numpy as jnp
from jax import lax
from jax.experimental import pallas as pl
from jax.experimental.pallas import tpu as pltpu
from jax.sharding import PartitionSpec as P

HD = 128
BLK = 16
GROUP = 16
NREQ = 16
LANES = GROUP * NREQ
STAT = 16
LOW = -1e30
FACTOR = 1.0 / math.sqrt(HD)
BF = jnp.bfloat16
F32 = jnp.float32


def vmem():
    return pl.BlockSpec(memory_space=pltpu.VMEM)


def dot(a, b, dims):
    return lax.dot_general(a, b, (dims, ((), ())), preferred_element_type=F32)


def rows_of(queries):
    return jnp.concatenate([queries[:, h * HD : (h + 1) * HD] for h in range(GROUP)], axis=0)


def stat_rows(peak, total, rows):
    place = lax.broadcasted_iota(jnp.int32, (rows, peak.shape[1]), 0)
    return jnp.where(place == 0, peak, jnp.where(place == 1, total, 0.0))


def packed_stats(peak, total):
    hi = peak.astype(BF).astype(F32)
    rest = peak - hi
    mid = rest.astype(BF).astype(F32)
    low = rest - mid
    total_hi = total.astype(BF).astype(F32)
    total_low = total - total_hi
    place = lax.broadcasted_iota(jnp.int32, (STAT, peak.shape[1]), 0)
    packed = jnp.zeros((STAT, peak.shape[1]), F32)
    for row, part in enumerate((hi, mid, low, total_hi, total_low)):
        packed = jnp.where(place == row, part, packed)
    return packed.astype(BF)


def unpacked_stats(packed):
    rows = packed.astype(F32)
    peak = rows[0:1] + (rows[1:2] + rows[2:3])
    total = rows[3:4] + rows[4:5]
    return peak, total


def store_packed(ref, weighted, peak, total):
    ref[0:HD, :] = weighted.astype(BF)
    ref[HD : HD + STAT, :] = packed_stats(peak, total)


def kv_kernel(x_ref, w_ref, out0, out1, out2, out3, x_buf, w_buf, sems):
    sec_id = lax.axis_index("sec")
    rows = out0.shape[0]
    copies = (
        pltpu.make_async_copy(w_ref, w_buf, sems.at[0]),
        pltpu.make_async_copy(x_ref, x_buf, sems.at[1]),
    )
    for copy in copies:
        copy.start()
    for copy in copies:
        copy.wait()
    for flip, out in enumerate((out0, out1, out2, out3)):
        start = pl.multiple_of((sec_id ^ flip) * rows, rows)
        out[...] = dot(x_buf[pl.ds(start, rows), :], w_buf[...], ((1,), (0,))).astype(BF)


def sum_kernel(own_ref, a_ref, b_ref, c_ref, out_ref):
    summed = (own_ref[...].astype(F32) + a_ref[...].astype(F32)) + (
        b_ref[...].astype(F32) + c_ref[...].astype(F32)
    )
    out_ref[...] = summed.astype(BF)


def cached_kernel(
    owner_ref, slot_ref, len_ref, ctx_ref, q_ref, cache_ref, weighted_ref, stats_ref, live_ref
):
    sec_id, req_id = lax.axis_index("sec"), lax.axis_index("req")
    count = cache_ref.shape[1]
    position = lax.broadcasted_iota(jnp.int32, (GROUP, count), 1) + sec_id * count
    lane = lax.broadcasted_iota(jnp.int32, (GROUP, LANES), 1)
    head = lax.broadcasted_iota(jnp.int32, (GROUP, LANES), 0)
    weighted = jnp.zeros((HD, LANES), F32)
    peaks = jnp.full((1, LANES), LOW, F32)
    totals = jnp.zeros((1, LANES), F32)
    for slot in range(2):
        queries = jnp.concatenate(
            [q_ref[slot : slot + 1, h * HD : (h + 1) * HD] for h in range(GROUP)], axis=0
        )
        live = position < ctx_ref[0:1, slot : slot + 1]
        scores = dot(queries, cache_ref[slot, :, 0:HD], ((1,), (1,))) * FACTOR
        scores = jnp.where(live, scores, LOW)
        peak = jnp.max(scores, axis=1, keepdims=True)
        weights = jnp.where(live, jnp.exp(scores - peak), 0.0)
        total = jnp.sum(weights, axis=1, keepdims=True)
        summed = dot(weights.astype(BF), cache_ref[slot, :, HD : 2 * HD], ((1,), (0,)))
        lane_of = lane == head * NREQ + req_id * 2 + slot
        spread = lane_of.astype(BF)
        high = summed.astype(BF)
        low = (summed - high.astype(F32)).astype(BF)
        weighted = weighted + dot(high, spread, ((0,), (0,))) + dot(low, spread, ((0,), (0,)))
        peaks = jnp.maximum(
            peaks, jnp.max(jnp.where(lane_of, peak, LOW), axis=0, keepdims=True)
        )
        totals = totals + jnp.sum(jnp.where(lane_of, total, 0.0), axis=0, keepdims=True)
    weighted_ref[...] = weighted
    stats_ref[...] = stat_rows(peaks, totals, 8)

    rows, blocks = live_ref.shape[0], owner_ref.shape[1]
    first = (req_id * lax.axis_size("sec") + sec_id) * (rows // BLK)
    token = lax.broadcasted_iota(jnp.int32, (rows, blocks), 0)
    block = lax.broadcasted_iota(jnp.int32, (rows, blocks), 1)
    mine = block == token // BLK + first
    holder = owner_ref[...] * 2 + slot_ref[...]
    holder = jnp.sum(jnp.where(mine, holder, 0).astype(F32), axis=1, keepdims=True)
    length = jnp.sum(jnp.where(mine, len_ref[...], 0).astype(F32), axis=1, keepdims=True)
    lane = lax.broadcasted_iota(jnp.int32, (rows, LANES), 1) % NREQ
    place = lax.broadcasted_iota(jnp.int32, (rows, LANES), 0) % BLK
    live = (lane.astype(F32) == holder) & (place.astype(F32) < length)
    live_ref[...] = live.astype(F32)


def place_kernel(mine_ref, other_ref, out_ref):
    req_id = lax.axis_index("req")
    place = lax.broadcasted_iota(jnp.int32, (NREQ, 2), 0)
    row = lax.broadcasted_iota(jnp.int32, (NREQ, 2), 1)
    mine = (place == req_id * 2 + row).astype(BF)
    other = (place == (req_id ^ 1) * 2 + row).astype(BF)
    placed = dot(mine, mine_ref[...], ((1,), (0,))) + dot(other, other_ref[...], ((1,), (0,)))
    out_ref[...] = placed.astype(BF)


def prompt_kernel(q_ref, live_ref, kv_ref, cw_ref, cs_ref, kw_ref, ks_ref, send_ref):
    new_kv = kv_ref[...]
    queries = rows_of(q_ref[...])
    live = live_ref[...] > 0.5
    scores = dot(new_kv[:, 0:HD], queries, ((1,), (1,))) * FACTOR
    scores = jnp.where(live, scores, LOW)
    peak = jnp.max(scores, axis=0, keepdims=True)
    weights = jnp.where(live, jnp.exp(scores - peak), 0.0)
    total = jnp.sum(weights, axis=0, keepdims=True)
    weighted = dot(new_kv[:, HD : 2 * HD], weights.astype(BF), ((0,), (0,)))
    cached_peak, cached_total = cs_ref[0:1, :], cs_ref[1:2, :]
    joint = jnp.maximum(peak, cached_peak)
    scale, cached_scale = jnp.exp(peak - joint), jnp.exp(cached_peak - joint)
    weighted = weighted * scale + cw_ref[...] * cached_scale
    total = total * scale + cached_total * cached_scale
    kw_ref[...] = weighted
    ks_ref[...] = stat_rows(joint, total, 8)
    store_packed(send_ref, weighted, joint, total)


def joined(w_ref, s_ref, got_refs):
    peaks, totals = [s_ref[0:1, :]], [s_ref[1:2, :]]
    for got_ref in got_refs:
        peak, total = unpacked_stats(got_ref[HD : HD + STAT, :])
        peaks.append(peak)
        totals.append(total)
    joint = peaks[0]
    for peak in peaks[1:]:
        joint = jnp.maximum(joint, peak)
    scales = [jnp.exp(peak - joint) for peak in peaks]
    weighted, total = w_ref[...] * scales[0], totals[0] * scales[0]
    for got_ref, part, scale in zip(got_refs, totals[1:], scales[1:]):
        weighted = weighted + got_ref[0:HD, :].astype(F32) * scale
        total = total + part * scale
    return weighted, joint, total


def join_kernel(w_ref, s_ref, *refs):
    got_refs, (kw_ref, ks_ref, send_ref) = refs[:-3], refs[-3:]
    weighted, peak, total = joined(w_ref, s_ref, got_refs)
    kw_ref[...] = weighted
    ks_ref[...] = stat_rows(peak, total, 8)
    store_packed(send_ref, weighted, peak, total)


def far_kernel(first_ref, second_ref, kw_ref, ks_ref, send_ref):
    use_second = (lax.axis_index("req") % 2).astype(F32)
    peak, total = unpacked_stats(first_ref[HD : HD + STAT, :])
    peak_2, total_2 = unpacked_stats(second_ref[HD : HD + STAT, :])
    joint = jnp.maximum(peak, peak_2)
    scale, scale_2 = jnp.exp(peak - joint), jnp.exp(peak_2 - joint) * use_second
    weighted = first_ref[0:HD, :].astype(F32) * scale + second_ref[0:HD, :].astype(F32) * scale_2
    total = total * scale + total_2 * scale_2
    kw_ref[...] = weighted
    ks_ref[...] = stat_rows(joint, total, 8)
    store_packed(send_ref, weighted, joint, total)


def project_kernel(w_ref, s_ref, far_w_ref, far_s_ref, out_w_ref, got_ref, out_ref):
    weighted, peak, total = joined(w_ref, s_ref, (got_ref,))
    far_peak, far_total = far_s_ref[0:1, :], far_s_ref[1:2, :]
    joint = jnp.maximum(peak, far_peak)
    scale, far_scale = jnp.exp(peak - joint), jnp.exp(far_peak - joint)
    weighted = weighted * scale + far_w_ref[...] * far_scale
    total = total * scale + far_total * far_scale
    rows = (weighted / total).T.astype(BF)
    attended = jnp.concatenate(
        [rows[h * NREQ : (h + 1) * NREQ, :] for h in range(GROUP)], axis=1
    )
    out_ref[...] = dot(attended, out_w_ref[...], ((1,), (0,))).astype(BF)


def shape(dims, dtype):
    return jax.ShapeDtypeStruct(dims, dtype)


def call(kernel, ins, outs, name, flops=0, scratch=(), grant=32):
    moved = 0
    for _, value in ins:
        moved += value.size * value.dtype.itemsize
    return pl.pallas_call(
        kernel,
        out_shape=outs,
        in_specs=[spec for spec, _ in ins],
        out_specs=jax.tree.map(lambda _: vmem(), outs),
        scratch_shapes=scratch,
        compiler_params=pltpu.CompilerParams(vmem_limit_bytes=grant * 1024 * 1024),
        cost_estimate=pl.CostEstimate(flops=flops, bytes_accessed=moved, transcendentals=0),
        name=name,
    )(*[value for _, value in ins])


STATE = (shape((HD, LANES), F32), shape((8, LANES), F32), shape((HD + STAT, LANES), BF))


def on_device(prompt_x, w_kv, queries, cache, w_out, blk_owner, blk_slot, blk_len, ctx_len):
    sec_count = lax.axis_size("sec")
    req_count = lax.axis_size("req")
    req_id = lax.axis_index("req")
    rows = prompt_x.shape[0] // sec_count
    width = w_kv.shape[1]

    def over(value, sec_flip, req_flip):
        if req_flip == 0:
            return lax.ppermute(value, "sec", [(i, i ^ sec_flip) for i in range(sec_count)])
        if sec_flip == 0:
            return lax.ppermute(value, "req", [(i, i ^ req_flip) for i in range(req_count)])
        return over_cores(value, (sec_flip, req_flip), (sec_flip, req_flip))

    def over_cores(value, flips_0, flips_1):
        pairs = []
        for i in range(sec_count):
            for j in range(req_count):
                sec_flip, req_flip = flips_1 if j % 2 else flips_0
                pairs.append((i * req_count + j, (i ^ sec_flip) * req_count + (j ^ req_flip)))
        return lax.ppermute(value, ("sec", "req"), pairs)

    chunk = shape((rows, width), BF)
    hbm = pl.BlockSpec(memory_space=pltpu.HBM)
    other_queries = over(queries, 0, 1)
    chunks = call(
        kv_kernel,
        [(hbm, prompt_x), (hbm, w_kv)],
        (chunk, chunk, chunk, chunk),
        "new_kv",
        flops=2 * prompt_x.size * width,
        scratch=(
            pltpu.VMEM(prompt_x.shape, BF),
            pltpu.VMEM(w_kv.shape, BF),
            pltpu.SemaphoreType.DMA((2,)),
        ),
        grant=52,
    )
    chunks, other_queries = lax.optimization_barrier((chunks, other_queries))

    gathered = call(
        place_kernel,
        [(vmem(), queries), (vmem(), other_queries)],
        shape((NREQ, queries.shape[1]), BF),
        "place",
    )
    gathered = gathered + over(gathered, 0, 2)
    arrived = [over(chunks[flip], flip, 0) for flip in (3, 2, 1)]
    gathered = gathered + over(gathered, 0, 6)
    cached_weighted, cached_stats, live = call(
        cached_kernel,
        [
            (vmem(), blk_owner.reshape(1, -1)),
            (vmem(), blk_slot.reshape(1, -1)),
            (vmem(), blk_len.reshape(1, -1)),
            (vmem(), ctx_len.reshape(1, -1)),
            (vmem(), queries),
            (vmem(), cache[:, :, 0, :]),
        ],
        (shape((HD, LANES), F32), shape((8, LANES), F32), shape((rows, LANES), F32)),
        "cached",
        flops=2 * 4 * cache.shape[1] * HD * LANES,
    )
    new_kv = call(
        sum_kernel, [(vmem(), value) for value in (chunks[0], *arrived)], chunk, "kv_sum"
    )
    kept = call(
        prompt_kernel,
        [
            (vmem(), value)
            for value in (gathered, live, new_kv, cached_weighted, cached_stats)
        ],
        STATE,
        "prompt",
        flops=2 * 2 * rows * HD * LANES,
    )
    for name, moves in (
        ("join_core", ((0, 1),)),
        ("join_near", ((1, 2), (1, 0), (0, 2))),
    ):
        got = [over(kept[2], *flips) for flips in moves]
        kept = call(
            join_kernel, [(vmem(), value) for value in (kept[0], kept[1], *got)], STATE, name
        )
    got = [
        over_cores(kept[2], (0, 6), flips) for flips in ((2, 0), (2, 6))
    ]
    far = call(far_kernel, [(vmem(), value) for value in got], STATE, "join_far")
    columns = w_out.shape[1]
    partial_out = call(
        project_kernel,
        [
            (vmem(), value)
            for value in (kept[0], kept[1], far[0], far[1], w_out, over(far[2], 0, 1))
        ],
        shape((NREQ, columns), BF),
        "project",
        flops=2 * w_out.size * NREQ,
    )
    head_count = lax.axis_size("head")
    pieces = partial_out.reshape(head_count, NREQ // head_count, columns)
    pieces = lax.all_to_all(pieces, "head", 0, 0, tiled=True)
    return jnp.sum(pieces.astype(F32), axis=0).astype(BF)


def solution(mesh):
    return jax.shard_map(
        on_device,
        mesh=mesh,
        in_specs=(
            P("req", "sec"),
            P("sec", "head"),
            P("req", "head"),
            P("req", "sec", "head", None),
            P("head", ("sec", "req")),
            P(),
            P(),
            P(),
            P("req"),
        ),
        out_specs=P("head", ("sec", "req")),
        check_vma=False,
    )
```

```python
import math

import jax
import jax.numpy as jnp
from jax import lax
from jax.experimental import pallas as pl
from jax.experimental.pallas import tpu as pltpu
from jax.sharding import PartitionSpec as P

HD = 128
BLK = 16
GROUP = 16
NREQ = 16
LANES = GROUP * NREQ
STAT = 16
LOW = -1e30
FACTOR = 1.0 / math.sqrt(HD)
BF = jnp.bfloat16
F32 = jnp.float32


def vmem():
    return pl.BlockSpec(memory_space=pltpu.VMEM)


def dot(a, b, dims):
    return lax.dot_general(a, b, (dims, ((), ())), preferred_element_type=F32)


def rows_of(queries):
    return jnp.concatenate([queries[:, h * HD : (h + 1) * HD] for h in range(GROUP)], axis=0)


def stat_rows(peak, total, rows):
    place = lax.broadcasted_iota(jnp.int32, (rows, peak.shape[1]), 0)
    return jnp.where(place == 0, peak, jnp.where(place == 1, total, 0.0))


def packed_stats(peak, total):
    hi = peak.astype(BF).astype(F32)
    rest = peak - hi
    mid = rest.astype(BF).astype(F32)
    low = rest - mid
    total_hi = total.astype(BF).astype(F32)
    total_low = total - total_hi
    place = lax.broadcasted_iota(jnp.int32, (STAT, peak.shape[1]), 0)
    packed = jnp.zeros((STAT, peak.shape[1]), F32)
    for row, part in enumerate((hi, mid, low, total_hi, total_low)):
        packed = jnp.where(place == row, part, packed)
    return packed.astype(BF)


def unpacked_stats(packed):
    rows = packed.astype(F32)
    peak = rows[0:1] + (rows[1:2] + rows[2:3])
    total = rows[3:4] + rows[4:5]
    return peak, total


def store_packed(ref, weighted, peak, total):
    ref[0:HD, :] = weighted.astype(BF)
    ref[HD : HD + STAT, :] = packed_stats(peak, total)


def kv_kernel(x_ref, w_ref, out0, out1, out2, out3):
    sec_id = lax.axis_index("sec")
    rows = out0.shape[0]
    for flip, out in enumerate((out0, out1, out2, out3)):
        start = pl.multiple_of((sec_id ^ flip) * rows, rows)
        out[...] = dot(x_ref[pl.ds(start, rows), :], w_ref[...], ((1,), (0,))).astype(BF)


def sum_kernel(own_ref, a_ref, b_ref, c_ref, out_ref):
    summed = (own_ref[...].astype(F32) + a_ref[...].astype(F32)) + (
        b_ref[...].astype(F32) + c_ref[...].astype(F32)
    )
    out_ref[...] = summed.astype(BF)


def cached_kernel(
    owner_ref, slot_ref, len_ref, ctx_ref, q_ref, cache_ref, weighted_ref, stats_ref, live_ref
):
    sec_id, req_id = lax.axis_index("sec"), lax.axis_index("req")
    count = cache_ref.shape[1]
    position = lax.broadcasted_iota(jnp.int32, (GROUP, count), 1) + sec_id * count
    lane = lax.broadcasted_iota(jnp.int32, (GROUP, LANES), 1)
    head = lax.broadcasted_iota(jnp.int32, (GROUP, LANES), 0)
    weighted = jnp.zeros((HD, LANES), F32)
    peaks = jnp.full((1, LANES), LOW, F32)
    totals = jnp.zeros((1, LANES), F32)
    for slot in range(2):
        queries = jnp.concatenate(
            [q_ref[slot : slot + 1, h * HD : (h + 1) * HD] for h in range(GROUP)], axis=0
        )
        live = position < ctx_ref[0:1, slot : slot + 1]
        scores = dot(queries, cache_ref[slot, :, 0:HD], ((1,), (1,))) * FACTOR
        scores = jnp.where(live, scores, LOW)
        peak = jnp.max(scores, axis=1, keepdims=True)
        weights = jnp.where(live, jnp.exp(scores - peak), 0.0)
        total = jnp.sum(weights, axis=1, keepdims=True)
        summed = dot(weights.astype(BF), cache_ref[slot, :, HD : 2 * HD], ((1,), (0,)))
        lane_of = lane == head * NREQ + req_id * 2 + slot
        spread = lane_of.astype(BF)
        high = summed.astype(BF)
        low = (summed - high.astype(F32)).astype(BF)
        weighted = weighted + dot(high, spread, ((0,), (0,))) + dot(low, spread, ((0,), (0,)))
        peaks = jnp.maximum(
            peaks, jnp.max(jnp.where(lane_of, peak, LOW), axis=0, keepdims=True)
        )
        totals = totals + jnp.sum(jnp.where(lane_of, total, 0.0), axis=0, keepdims=True)
    weighted_ref[...] = weighted
    stats_ref[...] = stat_rows(peaks, totals, 8)

    rows, blocks = live_ref.shape[0], owner_ref.shape[1]
    first = (req_id * lax.axis_size("sec") + sec_id) * (rows // BLK)
    token = lax.broadcasted_iota(jnp.int32, (rows, blocks), 0)
    block = lax.broadcasted_iota(jnp.int32, (rows, blocks), 1)
    mine = block == token // BLK + first
    holder = owner_ref[...] * 2 + slot_ref[...]
    holder = jnp.sum(jnp.where(mine, holder, 0).astype(F32), axis=1, keepdims=True)
    length = jnp.sum(jnp.where(mine, len_ref[...], 0).astype(F32), axis=1, keepdims=True)
    lane = lax.broadcasted_iota(jnp.int32, (rows, LANES), 1) % NREQ
    place = lax.broadcasted_iota(jnp.int32, (rows, LANES), 0) % BLK
    live = (lane.astype(F32) == holder) & (place.astype(F32) < length)
    live_ref[...] = live.astype(F32)


def place_kernel(mine_ref, out_ref):
    place = lax.broadcasted_iota(jnp.int32, (NREQ, 2), 0)
    row = lax.broadcasted_iota(jnp.int32, (NREQ, 2), 1)
    mine = (place == lax.axis_index("req") * 2 + row).astype(BF)
    out_ref[...] = dot(mine, mine_ref[...], ((1,), (0,))).astype(BF)


def prompt_kernel(q_ref, live_ref, kv_ref, cw_ref, cs_ref, kw_ref, ks_ref, send_ref):
    new_kv = kv_ref[...]
    queries = rows_of(q_ref[...])
    live = live_ref[...] > 0.5
    scores = dot(new_kv[:, 0:HD], queries, ((1,), (1,))) * FACTOR
    scores = jnp.where(live, scores, LOW)
    peak = jnp.max(scores, axis=0, keepdims=True)
    weights = jnp.where(live, jnp.exp(scores - peak), 0.0)
    total = jnp.sum(weights, axis=0, keepdims=True)
    weighted = dot(new_kv[:, HD : 2 * HD], weights.astype(BF), ((0,), (0,)))
    cached_peak, cached_total = cs_ref[0:1, :], cs_ref[1:2, :]
    joint = jnp.maximum(peak, cached_peak)
    scale, cached_scale = jnp.exp(peak - joint), jnp.exp(cached_peak - joint)
    weighted = weighted * scale + cw_ref[...] * cached_scale
    total = total * scale + cached_total * cached_scale
    kw_ref[...] = weighted
    ks_ref[...] = stat_rows(joint, total, 8)
    store_packed(send_ref, weighted, joint, total)


def joined(w_ref, s_ref, got_refs):
    peaks, totals = [s_ref[0:1, :]], [s_ref[1:2, :]]
    for got_ref in got_refs:
        peak, total = unpacked_stats(got_ref[HD : HD + STAT, :])
        peaks.append(peak)
        totals.append(total)
    joint = peaks[0]
    for peak in peaks[1:]:
        joint = jnp.maximum(joint, peak)
    scales = [jnp.exp(peak - joint) for peak in peaks]
    weighted, total = w_ref[...] * scales[0], totals[0] * scales[0]
    for got_ref, part, scale in zip(got_refs, totals[1:], scales[1:]):
        weighted = weighted + got_ref[0:HD, :].astype(F32) * scale
        total = total + part * scale
    return weighted, joint, total


def join_kernel(w_ref, s_ref, *refs):
    got_refs, (kw_ref, ks_ref, send_ref) = refs[:-3], refs[-3:]
    weighted, peak, total = joined(w_ref, s_ref, got_refs)
    kw_ref[...] = weighted
    ks_ref[...] = stat_rows(peak, total, 8)
    store_packed(send_ref, weighted, peak, total)


def far_kernel(first_ref, second_ref, kw_ref, ks_ref, send_ref):
    use_second = (lax.axis_index("req") % 2).astype(F32)
    peak, total = unpacked_stats(first_ref[HD : HD + STAT, :])
    peak_2, total_2 = unpacked_stats(second_ref[HD : HD + STAT, :])
    joint = jnp.maximum(peak, peak_2)
    scale, scale_2 = jnp.exp(peak - joint), jnp.exp(peak_2 - joint) * use_second
    weighted = first_ref[0:HD, :].astype(F32) * scale + second_ref[0:HD, :].astype(F32) * scale_2
    total = total * scale + total_2 * scale_2
    kw_ref[...] = weighted
    ks_ref[...] = stat_rows(joint, total, 8)
    store_packed(send_ref, weighted, joint, total)


def project_kernel(w_ref, s_ref, far_w_ref, far_s_ref, out_w_ref, got_ref, out_ref):
    weighted, peak, total = joined(w_ref, s_ref, (got_ref,))
    far_peak, far_total = far_s_ref[0:1, :], far_s_ref[1:2, :]
    joint = jnp.maximum(peak, far_peak)
    scale, far_scale = jnp.exp(peak - joint), jnp.exp(far_peak - joint)
    weighted = weighted * scale + far_w_ref[...] * far_scale
    total = total * scale + far_total * far_scale
    rows = (weighted / total).T.astype(BF)
    attended = jnp.concatenate(
        [rows[h * NREQ : (h + 1) * NREQ, :] for h in range(GROUP)], axis=1
    )
    out_ref[...] = dot(attended, out_w_ref[...], ((1,), (0,))).astype(BF)


def shape(dims, dtype):
    return jax.ShapeDtypeStruct(dims, dtype)


def call(kernel, ins, outs, name, flops=0, scratch=(), grant=32):
    moved = 0
    for _, value in ins:
        moved += value.size * value.dtype.itemsize
    return pl.pallas_call(
        kernel,
        out_shape=outs,
        in_specs=[spec for spec, _ in ins],
        out_specs=jax.tree.map(lambda _: vmem(), outs),
        scratch_shapes=scratch,
        compiler_params=pltpu.CompilerParams(vmem_limit_bytes=grant * 1024 * 1024),
        cost_estimate=pl.CostEstimate(flops=flops, bytes_accessed=moved, transcendentals=0),
        name=name,
    )(*[value for _, value in ins])


STATE = (shape((HD, LANES), F32), shape((8, LANES), F32), shape((HD + STAT, LANES), BF))


def on_device(prompt_x, w_kv, queries, cache, w_out, blk_owner, blk_slot, blk_len, ctx_len):
    sec_count = lax.axis_size("sec")
    req_count = lax.axis_size("req")
    req_id = lax.axis_index("req")
    rows = prompt_x.shape[0] // sec_count
    width = w_kv.shape[1]

    def over(value, sec_flip, req_flip):
        if req_flip == 0:
            return lax.ppermute(value, "sec", [(i, i ^ sec_flip) for i in range(sec_count)])
        if sec_flip == 0:
            return lax.ppermute(value, "req", [(i, i ^ req_flip) for i in range(req_count)])
        return over_cores(value, (sec_flip, req_flip), (sec_flip, req_flip))

    def over_cores(value, flips_0, flips_1):
        pairs = []
        for i in range(sec_count):
            for j in range(req_count):
                sec_flip, req_flip = flips_1 if j % 2 else flips_0
                pairs.append((i * req_count + j, (i ^ sec_flip) * req_count + (j ^ req_flip)))
        return lax.ppermute(value, ("sec", "req"), pairs)

    chunk = shape((rows, width), BF)
    gathered = call(
        place_kernel,
        [(vmem(), queries)],
        shape((NREQ, queries.shape[1]), BF),
        "place",
        flops=2_000_000_000,
    )
    gathered = gathered + over(gathered, 0, 1)
    gathered = gathered + over(gathered, 0, 2)
    chunks = call(
        kv_kernel,
        [(vmem(), prompt_x), (vmem(), w_kv)],
        (chunk, chunk, chunk, chunk),
        "new_kv",
        flops=2 * prompt_x.size * width,
    )
    arrived = [over(chunks[flip], flip, 0) for flip in (3, 2, 1)]
    gathered = gathered + over(gathered, 0, 6)
    cached_weighted, cached_stats, live = call(
        cached_kernel,
        [
            (vmem(), blk_owner.reshape(1, -1)),
            (vmem(), blk_slot.reshape(1, -1)),
            (vmem(), blk_len.reshape(1, -1)),
            (vmem(), ctx_len.reshape(1, -1)),
            (vmem(), queries),
            (vmem(), cache[:, :, 0, :]),
        ],
        (shape((HD, LANES), F32), shape((8, LANES), F32), shape((rows, LANES), F32)),
        "cached",
        flops=2 * 4 * cache.shape[1] * HD * LANES,
    )
    new_kv = call(
        sum_kernel, [(vmem(), value) for value in (chunks[0], *arrived)], chunk, "kv_sum"
    )
    kept = call(
        prompt_kernel,
        [
            (vmem(), value)
            for value in (gathered, live, new_kv, cached_weighted, cached_stats)
        ],
        STATE,
        "prompt",
        flops=2 * 2 * rows * HD * LANES,
    )
    for name, moves in (
        ("join_core", ((0, 1),)),
        ("join_near", ((1, 0), (0, 2), (1, 2))),
    ):
        got = [over(kept[2], *flips) for flips in moves]
        kept = call(
            join_kernel, [(vmem(), value) for value in (kept[0], kept[1], *got)], STATE, name
        )
    got = [
        over_cores(kept[2], (0, 6), flips) for flips in ((2, 0), (2, 6))
    ]
    far = call(far_kernel, [(vmem(), value) for value in got], STATE, "join_far")
    columns = w_out.shape[1]
    partial_out = call(
        project_kernel,
        [
            (vmem(), value)
            for value in (kept[0], kept[1], far[0], far[1], w_out, over(far[2], 0, 1))
        ],
        shape((NREQ, columns), BF),
        "project",
        flops=2 * w_out.size * NREQ,
    )
    head_count = lax.axis_size("head")
    pieces = partial_out.reshape(head_count, NREQ // head_count, columns)
    pieces = lax.all_to_all(pieces, "head", 0, 0, tiled=True)
    return jnp.sum(pieces.astype(F32), axis=0).astype(BF)


def solution(mesh):
    return jax.shard_map(
        on_device,
        mesh=mesh,
        in_specs=(
            P("req", "sec"),
            P("sec", "head"),
            P("req", "head"),
            P("req", "sec", "head", None),
            P("head", ("sec", "req")),
            P(),
            P(),
            P(),
            P("req"),
        ),
        out_specs=P("head", ("sec", "req")),
        check_vma=False,
    )
```

```python
import math

import jax
import jax.numpy as jnp
from jax import lax
from jax.experimental import pallas as pl
from jax.experimental.pallas import tpu as pltpu
from jax.sharding import PartitionSpec as P

HD = 128
BLK = 16
GROUP = 16
NREQ = 16
LANES = GROUP * NREQ
STAT = 16
LOW = -1e30
FACTOR = 1.0 / math.sqrt(HD)
BF = jnp.bfloat16
F32 = jnp.float32


def vmem():
    return pl.BlockSpec(memory_space=pltpu.VMEM)


def dot(a, b, dims):
    return lax.dot_general(a, b, (dims, ((), ())), preferred_element_type=F32)


def rows_of(queries):
    return jnp.concatenate([queries[:, h * HD : (h + 1) * HD] for h in range(GROUP)], axis=0)


def stat_rows(peak, total, rows):
    place = lax.broadcasted_iota(jnp.int32, (rows, peak.shape[1]), 0)
    return jnp.where(place == 0, peak, jnp.where(place == 1, total, 0.0))


def packed_stats(peak, total):
    hi = peak.astype(BF).astype(F32)
    rest = peak - hi
    mid = rest.astype(BF).astype(F32)
    low = rest - mid
    total_hi = total.astype(BF).astype(F32)
    total_low = total - total_hi
    place = lax.broadcasted_iota(jnp.int32, (STAT, peak.shape[1]), 0)
    packed = jnp.zeros((STAT, peak.shape[1]), F32)
    for row, part in enumerate((hi, mid, low, total_hi, total_low)):
        packed = jnp.where(place == row, part, packed)
    return packed.astype(BF)


def unpacked_stats(packed):
    rows = packed.astype(F32)
    peak = rows[0:1] + (rows[1:2] + rows[2:3])
    total = rows[3:4] + rows[4:5]
    return peak, total


def store_packed(ref, weighted, peak, total):
    ref[0:HD, :] = weighted.astype(BF)
    ref[HD : HD + STAT, :] = packed_stats(peak, total)


def kv_kernel(x_ref, w_ref, out0, out1, out2, out3):
    sec_id = lax.axis_index("sec")
    rows = out0.shape[0]
    for flip, out in enumerate((out0, out1, out2, out3)):
        start = pl.multiple_of((sec_id ^ flip) * rows, rows)
        out[...] = dot(x_ref[pl.ds(start, rows), :], w_ref[...], ((1,), (0,))).astype(BF)


def sum_kernel(own_ref, a_ref, b_ref, c_ref, out_ref):
    summed = (own_ref[...].astype(F32) + a_ref[...].astype(F32)) + (
        b_ref[...].astype(F32) + c_ref[...].astype(F32)
    )
    out_ref[...] = summed.astype(BF)


def cached_kernel(
    owner_ref, slot_ref, len_ref, ctx_ref, q_ref, cache_ref, weighted_ref, stats_ref, live_ref
):
    sec_id, req_id = lax.axis_index("sec"), lax.axis_index("req")
    count = cache_ref.shape[1]
    position = lax.broadcasted_iota(jnp.int32, (GROUP, count), 1) + sec_id * count
    lane = lax.broadcasted_iota(jnp.int32, (GROUP, LANES), 1)
    head = lax.broadcasted_iota(jnp.int32, (GROUP, LANES), 0)
    weighted = jnp.zeros((HD, LANES), F32)
    peaks = jnp.full((1, LANES), LOW, F32)
    totals = jnp.zeros((1, LANES), F32)
    for slot in range(2):
        queries = jnp.concatenate(
            [q_ref[slot : slot + 1, h * HD : (h + 1) * HD] for h in range(GROUP)], axis=0
        )
        live = position < ctx_ref[0:1, slot : slot + 1]
        scores = dot(queries, cache_ref[slot, :, 0:HD], ((1,), (1,))) * FACTOR
        scores = jnp.where(live, scores, LOW)
        peak = jnp.max(scores, axis=1, keepdims=True)
        weights = jnp.where(live, jnp.exp(scores - peak), 0.0)
        total = jnp.sum(weights, axis=1, keepdims=True)
        summed = dot(weights.astype(BF), cache_ref[slot, :, HD : 2 * HD], ((1,), (0,)))
        lane_of = lane == head * NREQ + req_id * 2 + slot
        spread = lane_of.astype(BF)
        high = summed.astype(BF)
        low = (summed - high.astype(F32)).astype(BF)
        weighted = weighted + dot(high, spread, ((0,), (0,))) + dot(low, spread, ((0,), (0,)))
        peaks = jnp.maximum(
            peaks, jnp.max(jnp.where(lane_of, peak, LOW), axis=0, keepdims=True)
        )
        totals = totals + jnp.sum(jnp.where(lane_of, total, 0.0), axis=0, keepdims=True)
    weighted_ref[...] = weighted
    stats_ref[...] = stat_rows(peaks, totals, 8)

    rows, blocks = live_ref.shape[0], owner_ref.shape[1]
    first = (req_id * lax.axis_size("sec") + sec_id) * (rows // BLK)
    token = lax.broadcasted_iota(jnp.int32, (rows, blocks), 0)
    block = lax.broadcasted_iota(jnp.int32, (rows, blocks), 1)
    mine = block == token // BLK + first
    holder = owner_ref[...] * 2 + slot_ref[...]
    holder = jnp.sum(jnp.where(mine, holder, 0).astype(F32), axis=1, keepdims=True)
    length = jnp.sum(jnp.where(mine, len_ref[...], 0).astype(F32), axis=1, keepdims=True)
    lane = lax.broadcasted_iota(jnp.int32, (rows, LANES), 1) % NREQ
    place = lax.broadcasted_iota(jnp.int32, (rows, LANES), 0) % BLK
    live = (lane.astype(F32) == holder) & (place.astype(F32) < length)
    live_ref[...] = live.astype(F32)


def placed(rows, holder):
    place = lax.broadcasted_iota(jnp.int32, (NREQ, 2), 0)
    row = lax.broadcasted_iota(jnp.int32, (NREQ, 2), 1)
    return dot((place == holder * 2 + row).astype(BF), rows, ((1,), (0,)))


def place_mine_kernel(mine_ref, out_ref):
    out_ref[...] = placed(mine_ref[...], lax.axis_index("req")).astype(BF)


def place_other_kernel(so_far_ref, other_ref, out_ref):
    other = placed(other_ref[...], lax.axis_index("req") ^ 1)
    out_ref[...] = (so_far_ref[...].astype(F32) + other).astype(BF)


def prompt_kernel(q_ref, live_ref, kv_ref, cw_ref, cs_ref, kw_ref, ks_ref, send_ref):
    new_kv = kv_ref[...]
    queries = rows_of(q_ref[...])
    live = live_ref[...] > 0.5
    scores = dot(new_kv[:, 0:HD], queries, ((1,), (1,))) * FACTOR
    scores = jnp.where(live, scores, LOW)
    peak = jnp.max(scores, axis=0, keepdims=True)
    weights = jnp.where(live, jnp.exp(scores - peak), 0.0)
    total = jnp.sum(weights, axis=0, keepdims=True)
    weighted = dot(new_kv[:, HD : 2 * HD], weights.astype(BF), ((0,), (0,)))
    cached_peak, cached_total = cs_ref[0:1, :], cs_ref[1:2, :]
    joint = jnp.maximum(peak, cached_peak)
    scale, cached_scale = jnp.exp(peak - joint), jnp.exp(cached_peak - joint)
    weighted = weighted * scale + cw_ref[...] * cached_scale
    total = total * scale + cached_total * cached_scale
    kw_ref[...] = weighted
    ks_ref[...] = stat_rows(joint, total, 8)
    store_packed(send_ref, weighted, joint, total)


def joined(w_ref, s_ref, got_refs):
    peaks, totals = [s_ref[0:1, :]], [s_ref[1:2, :]]
    for got_ref in got_refs:
        peak, total = unpacked_stats(got_ref[HD : HD + STAT, :])
        peaks.append(peak)
        totals.append(total)
    joint = peaks[0]
    for peak in peaks[1:]:
        joint = jnp.maximum(joint, peak)
    scales = [jnp.exp(peak - joint) for peak in peaks]
    weighted, total = w_ref[...] * scales[0], totals[0] * scales[0]
    for got_ref, part, scale in zip(got_refs, totals[1:], scales[1:]):
        weighted = weighted + got_ref[0:HD, :].astype(F32) * scale
        total = total + part * scale
    return weighted, joint, total


def join_kernel(w_ref, s_ref, *refs):
    got_refs, (kw_ref, ks_ref, send_ref) = refs[:-3], refs[-3:]
    weighted, peak, total = joined(w_ref, s_ref, got_refs)
    kw_ref[...] = weighted
    ks_ref[...] = stat_rows(peak, total, 8)
    store_packed(send_ref, weighted, peak, total)


def far_kernel(first_ref, second_ref, kw_ref, ks_ref, send_ref):
    use_second = (lax.axis_index("req") % 2).astype(F32)
    peak, total = unpacked_stats(first_ref[HD : HD + STAT, :])
    peak_2, total_2 = unpacked_stats(second_ref[HD : HD + STAT, :])
    joint = jnp.maximum(peak, peak_2)
    scale, scale_2 = jnp.exp(peak - joint), jnp.exp(peak_2 - joint) * use_second
    weighted = first_ref[0:HD, :].astype(F32) * scale + second_ref[0:HD, :].astype(F32) * scale_2
    total = total * scale + total_2 * scale_2
    kw_ref[...] = weighted
    ks_ref[...] = stat_rows(joint, total, 8)
    store_packed(send_ref, weighted, joint, total)


def project_kernel(w_ref, s_ref, far_w_ref, far_s_ref, out_w_ref, got_ref, out_ref):
    weighted, peak, total = joined(w_ref, s_ref, (got_ref,))
    far_peak, far_total = far_s_ref[0:1, :], far_s_ref[1:2, :]
    joint = jnp.maximum(peak, far_peak)
    scale, far_scale = jnp.exp(peak - joint), jnp.exp(far_peak - joint)
    weighted = weighted * scale + far_w_ref[...] * far_scale
    total = total * scale + far_total * far_scale
    rows = (weighted / total).T.astype(BF)
    attended = jnp.concatenate(
        [rows[h * NREQ : (h + 1) * NREQ, :] for h in range(GROUP)], axis=1
    )
    out_ref[...] = dot(attended, out_w_ref[...], ((1,), (0,))).astype(BF)


def shape(dims, dtype):
    return jax.ShapeDtypeStruct(dims, dtype)


def call(kernel, ins, outs, name, flops=0, scratch=(), grant=32):
    moved = 0
    for _, value in ins:
        moved += value.size * value.dtype.itemsize
    return pl.pallas_call(
        kernel,
        out_shape=outs,
        in_specs=[spec for spec, _ in ins],
        out_specs=jax.tree.map(lambda _: vmem(), outs),
        scratch_shapes=scratch,
        compiler_params=pltpu.CompilerParams(vmem_limit_bytes=grant * 1024 * 1024),
        cost_estimate=pl.CostEstimate(flops=flops, bytes_accessed=moved, transcendentals=0),
        name=name,
    )(*[value for _, value in ins])


STATE = (shape((HD, LANES), F32), shape((8, LANES), F32), shape((HD + STAT, LANES), BF))


def on_device(prompt_x, w_kv, queries, cache, w_out, blk_owner, blk_slot, blk_len, ctx_len):
    sec_count = lax.axis_size("sec")
    req_count = lax.axis_size("req")
    req_id = lax.axis_index("req")
    rows = prompt_x.shape[0] // sec_count
    width = w_kv.shape[1]

    def over(value, sec_flip, req_flip):
        if req_flip == 0:
            return lax.ppermute(value, "sec", [(i, i ^ sec_flip) for i in range(sec_count)])
        if sec_flip == 0:
            return lax.ppermute(value, "req", [(i, i ^ req_flip) for i in range(req_count)])
        return over_cores(value, (sec_flip, req_flip), (sec_flip, req_flip))

    def over_cores(value, flips_0, flips_1):
        pairs = []
        for i in range(sec_count):
            for j in range(req_count):
                sec_flip, req_flip = flips_1 if j % 2 else flips_0
                pairs.append((i * req_count + j, (i ^ sec_flip) * req_count + (j ^ req_flip)))
        return lax.ppermute(value, ("sec", "req"), pairs)

    chunk = shape((rows, width), BF)
    everyone = shape((NREQ, queries.shape[1]), BF)
    other_queries = over(queries, 0, 1)
    gathered = call(
        place_mine_kernel, [(vmem(), queries)], everyone, "place_mine", flops=2_000_000_000
    )
    gathered = call(
        place_other_kernel, [(vmem(), gathered), (vmem(), other_queries)], everyone, "place_other"
    )
    gathered = gathered + over(gathered, 0, 2)
    chunks = call(
        kv_kernel,
        [(vmem(), prompt_x), (vmem(), w_kv)],
        (chunk, chunk, chunk, chunk),
        "new_kv",
        flops=2 * prompt_x.size * width,
    )
    arrived = [over(chunks[flip], flip, 0) for flip in (3, 2, 1)]
    gathered = gathered + over(gathered, 0, 6)
    cached_weighted, cached_stats, live = call(
        cached_kernel,
        [
            (vmem(), blk_owner.reshape(1, -1)),
            (vmem(), blk_slot.reshape(1, -1)),
            (vmem(), blk_len.reshape(1, -1)),
            (vmem(), ctx_len.reshape(1, -1)),
            (vmem(), queries),
            (vmem(), cache[:, :, 0, :]),
        ],
        (shape((HD, LANES), F32), shape((8, LANES), F32), shape((rows, LANES), F32)),
        "cached",
        flops=2 * 4 * cache.shape[1] * HD * LANES,
    )
    new_kv = call(
        sum_kernel, [(vmem(), value) for value in (chunks[0], *arrived)], chunk, "kv_sum"
    )
    kept = call(
        prompt_kernel,
        [
            (vmem(), value)
            for value in (gathered, live, new_kv, cached_weighted, cached_stats)
        ],
        STATE,
        "prompt",
        flops=2 * 2 * rows * HD * LANES,
    )
    for name, moves in (
        ("join_core", ((0, 1),)),
        ("join_near", ((0, 2), (0, 6), (0, 4))),
    ):
        got = [over(kept[2], *flips) for flips in moves]
        kept = call(
            join_kernel, [(vmem(), value) for value in (kept[0], kept[1], *got)], STATE, name
        )
    got = [
        over_cores(kept[2], (1, 0), flips) for flips in ((3, 0), (2, 0))
    ]
    far = call(far_kernel, [(vmem(), value) for value in got], STATE, "join_far")
    columns = w_out.shape[1]
    partial_out = call(
        project_kernel,
        [
            (vmem(), value)
            for value in (kept[0], kept[1], far[0], far[1], w_out, over(far[2], 0, 1))
        ],
        shape((NREQ, columns), BF),
        "project",
        flops=2 * w_out.size * NREQ,
    )
    head_count = lax.axis_size("head")
    pieces = partial_out.reshape(head_count, NREQ // head_count, columns)
    pieces = lax.all_to_all(pieces, "head", 0, 0, tiled=True)
    return jnp.sum(pieces.astype(F32), axis=0).astype(BF)


def solution(mesh):
    return jax.shard_map(
        on_device,
        mesh=mesh,
        in_specs=(
            P("req", "sec"),
            P("sec", "head"),
            P("req", "head"),
            P("req", "sec", "head", None),
            P("head", ("sec", "req")),
            P(),
            P(),
            P(),
            P("req"),
        ),
        out_specs=P("head", ("sec", "req")),
        check_vma=False,
    )
```

```python
import math

import jax
import jax.numpy as jnp
from jax import lax
from jax.experimental import pallas as pl
from jax.experimental.pallas import tpu as pltpu
from jax.sharding import PartitionSpec as P

HD = 128
BLK = 16
GROUP = 16
NREQ = 16
LANES = GROUP * NREQ
STAT = 16
LOW = -1e30
FACTOR = 1.0 / math.sqrt(HD)
BF = jnp.bfloat16
F32 = jnp.float32


def vmem():
    return pl.BlockSpec(memory_space=pltpu.VMEM)


def dot(a, b, dims):
    return lax.dot_general(a, b, (dims, ((), ())), preferred_element_type=F32)


def rows_of(queries):
    return jnp.concatenate([queries[:, h * HD : (h + 1) * HD] for h in range(GROUP)], axis=0)


def stat_rows(peak, total, rows):
    place = lax.broadcasted_iota(jnp.int32, (rows, peak.shape[1]), 0)
    return jnp.where(place == 0, peak, jnp.where(place == 1, total, 0.0))


def packed_stats(peak, total):
    hi = peak.astype(BF).astype(F32)
    rest = peak - hi
    mid = rest.astype(BF).astype(F32)
    low = rest - mid
    total_hi = total.astype(BF).astype(F32)
    total_low = total - total_hi
    place = lax.broadcasted_iota(jnp.int32, (STAT, peak.shape[1]), 0)
    packed = jnp.zeros((STAT, peak.shape[1]), F32)
    for row, part in enumerate((hi, mid, low, total_hi, total_low)):
        packed = jnp.where(place == row, part, packed)
    return packed.astype(BF)


def unpacked_stats(packed):
    rows = packed.astype(F32)
    peak = rows[0:1] + (rows[1:2] + rows[2:3])
    total = rows[3:4] + rows[4:5]
    return peak, total


def store_packed(ref, weighted, peak, total):
    ref[0:HD, :] = weighted.astype(BF)
    ref[HD : HD + STAT, :] = packed_stats(peak, total)


def kv_kernel(x_ref, w_ref, out0, out1, out2, out3):
    sec_id = lax.axis_index("sec")
    rows = out0.shape[0]
    for flip, out in enumerate((out0, out1, out2, out3)):
        start = pl.multiple_of((sec_id ^ flip) * rows, rows)
        out[...] = dot(x_ref[pl.ds(start, rows), :], w_ref[...], ((1,), (0,))).astype(BF)


def sum_kernel(own_ref, a_ref, b_ref, c_ref, out_ref):
    summed = (own_ref[...].astype(F32) + a_ref[...].astype(F32)) + (
        b_ref[...].astype(F32) + c_ref[...].astype(F32)
    )
    out_ref[...] = summed.astype(BF)


def cached_kernel(
    owner_ref, slot_ref, len_ref, ctx_ref, q_ref, cache_ref, weighted_ref, stats_ref, live_ref
):
    sec_id, req_id = lax.axis_index("sec"), lax.axis_index("req")
    count = cache_ref.shape[1]
    position = lax.broadcasted_iota(jnp.int32, (GROUP, count), 1) + sec_id * count
    lane = lax.broadcasted_iota(jnp.int32, (GROUP, LANES), 1)
    head = lax.broadcasted_iota(jnp.int32, (GROUP, LANES), 0)
    weighted = jnp.zeros((HD, LANES), F32)
    peaks = jnp.full((1, LANES), LOW, F32)
    totals = jnp.zeros((1, LANES), F32)
    for slot in range(2):
        queries = jnp.concatenate(
            [q_ref[slot : slot + 1, h * HD : (h + 1) * HD] for h in range(GROUP)], axis=0
        )
        live = position < ctx_ref[0:1, slot : slot + 1]
        scores = dot(queries, cache_ref[slot, :, 0:HD], ((1,), (1,))) * FACTOR
        scores = jnp.where(live, scores, LOW)
        peak = jnp.max(scores, axis=1, keepdims=True)
        weights = jnp.where(live, jnp.exp(scores - peak), 0.0)
        total = jnp.sum(weights, axis=1, keepdims=True)
        summed = dot(weights.astype(BF), cache_ref[slot, :, HD : 2 * HD], ((1,), (0,)))
        lane_of = lane == head * NREQ + req_id * 2 + slot
        spread = lane_of.astype(BF)
        high = summed.astype(BF)
        low = (summed - high.astype(F32)).astype(BF)
        weighted = weighted + dot(high, spread, ((0,), (0,))) + dot(low, spread, ((0,), (0,)))
        peaks = jnp.maximum(
            peaks, jnp.max(jnp.where(lane_of, peak, LOW), axis=0, keepdims=True)
        )
        totals = totals + jnp.sum(jnp.where(lane_of, total, 0.0), axis=0, keepdims=True)
    weighted_ref[...] = weighted
    stats_ref[...] = stat_rows(peaks, totals, 8)

    rows, blocks = live_ref.shape[0], owner_ref.shape[1]
    first = (req_id * lax.axis_size("sec") + sec_id) * (rows // BLK)
    token = lax.broadcasted_iota(jnp.int32, (rows, blocks), 0)
    block = lax.broadcasted_iota(jnp.int32, (rows, blocks), 1)
    mine = block == token // BLK + first
    holder = owner_ref[...] * 2 + slot_ref[...]
    holder = jnp.sum(jnp.where(mine, holder, 0).astype(F32), axis=1, keepdims=True)
    length = jnp.sum(jnp.where(mine, len_ref[...], 0).astype(F32), axis=1, keepdims=True)
    lane = lax.broadcasted_iota(jnp.int32, (rows, LANES), 1) % NREQ
    place = lax.broadcasted_iota(jnp.int32, (rows, LANES), 0) % BLK
    live = (lane.astype(F32) == holder) & (place.astype(F32) < length)
    live_ref[...] = live.astype(F32)


def placed(rows, holder):
    place = lax.broadcasted_iota(jnp.int32, (NREQ, 2), 0)
    row = lax.broadcasted_iota(jnp.int32, (NREQ, 2), 1)
    return dot((place == holder * 2 + row).astype(BF), rows, ((1,), (0,)))


def place_mine_kernel(mine_ref, out_ref):
    out_ref[...] = placed(mine_ref[...], lax.axis_index("req")).astype(BF)


def place_other_kernel(so_far_ref, other_ref, out_ref):
    other = placed(other_ref[...], lax.axis_index("req") ^ 1)
    out_ref[...] = (so_far_ref[...].astype(F32) + other).astype(BF)


def prompt_kernel(q_ref, live_ref, kv_ref, cw_ref, cs_ref, kw_ref, ks_ref, send_ref):
    new_kv = kv_ref[...]
    queries = rows_of(q_ref[...])
    live = live_ref[...] > 0.5
    scores = dot(new_kv[:, 0:HD], queries, ((1,), (1,))) * FACTOR
    scores = jnp.where(live, scores, LOW)
    peak = jnp.max(scores, axis=0, keepdims=True)
    weights = jnp.where(live, jnp.exp(scores - peak), 0.0)
    total = jnp.sum(weights, axis=0, keepdims=True)
    weighted = dot(new_kv[:, HD : 2 * HD], weights.astype(BF), ((0,), (0,)))
    cached_peak, cached_total = cs_ref[0:1, :], cs_ref[1:2, :]
    joint = jnp.maximum(peak, cached_peak)
    scale, cached_scale = jnp.exp(peak - joint), jnp.exp(cached_peak - joint)
    weighted = weighted * scale + cw_ref[...] * cached_scale
    total = total * scale + cached_total * cached_scale
    kw_ref[...] = weighted
    ks_ref[...] = stat_rows(joint, total, 8)
    store_packed(send_ref, weighted, joint, total)


def joined(w_ref, s_ref, got_refs):
    peaks, totals = [s_ref[0:1, :]], [s_ref[1:2, :]]
    for got_ref in got_refs:
        peak, total = unpacked_stats(got_ref[HD : HD + STAT, :])
        peaks.append(peak)
        totals.append(total)
    joint = peaks[0]
    for peak in peaks[1:]:
        joint = jnp.maximum(joint, peak)
    scales = [jnp.exp(peak - joint) for peak in peaks]
    weighted, total = w_ref[...] * scales[0], totals[0] * scales[0]
    for got_ref, part, scale in zip(got_refs, totals[1:], scales[1:]):
        weighted = weighted + got_ref[0:HD, :].astype(F32) * scale
        total = total + part * scale
    return weighted, joint, total


def join_kernel(w_ref, s_ref, *refs):
    got_refs, (kw_ref, ks_ref, send_ref) = refs[:-3], refs[-3:]
    weighted, peak, total = joined(w_ref, s_ref, got_refs)
    kw_ref[...] = weighted
    ks_ref[...] = stat_rows(peak, total, 8)
    store_packed(send_ref, weighted, peak, total)


def far_kernel(first_ref, second_ref, kw_ref, ks_ref, send_ref):
    use_second = (lax.axis_index("req") % 2).astype(F32)
    peak, total = unpacked_stats(first_ref[HD : HD + STAT, :])
    peak_2, total_2 = unpacked_stats(second_ref[HD : HD + STAT, :])
    joint = jnp.maximum(peak, peak_2)
    scale, scale_2 = jnp.exp(peak - joint), jnp.exp(peak_2 - joint) * use_second
    weighted = first_ref[0:HD, :].astype(F32) * scale + second_ref[0:HD, :].astype(F32) * scale_2
    total = total * scale + total_2 * scale_2
    kw_ref[...] = weighted
    ks_ref[...] = stat_rows(joint, total, 8)
    store_packed(send_ref, weighted, joint, total)


def project_kernel(w_ref, s_ref, far_w_ref, far_s_ref, out_w_ref, got_ref, out_ref):
    weighted, peak, total = joined(w_ref, s_ref, (got_ref,))
    far_peak, far_total = far_s_ref[0:1, :], far_s_ref[1:2, :]
    joint = jnp.maximum(peak, far_peak)
    scale, far_scale = jnp.exp(peak - joint), jnp.exp(far_peak - joint)
    weighted = weighted * scale + far_w_ref[...] * far_scale
    total = total * scale + far_total * far_scale
    rows = (weighted / total).T.astype(BF)
    attended = jnp.concatenate(
        [rows[h * NREQ : (h + 1) * NREQ, :] for h in range(GROUP)], axis=1
    )
    out_ref[...] = dot(attended, out_w_ref[...], ((1,), (0,))).astype(BF)


def shape(dims, dtype):
    return jax.ShapeDtypeStruct(dims, dtype)


def call(kernel, ins, outs, name, flops=0, scratch=(), grant=32):
    moved = 0
    for _, value in ins:
        moved += value.size * value.dtype.itemsize
    return pl.pallas_call(
        kernel,
        out_shape=outs,
        in_specs=[spec for spec, _ in ins],
        out_specs=jax.tree.map(lambda _: vmem(), outs),
        scratch_shapes=scratch,
        compiler_params=pltpu.CompilerParams(vmem_limit_bytes=grant * 1024 * 1024),
        cost_estimate=pl.CostEstimate(flops=flops, bytes_accessed=moved, transcendentals=0),
        name=name,
    )(*[value for _, value in ins])


STATE = (shape((HD, LANES), F32), shape((8, LANES), F32), shape((HD + STAT, LANES), BF))


def on_device(prompt_x, w_kv, queries, cache, w_out, blk_owner, blk_slot, blk_len, ctx_len):
    sec_count = lax.axis_size("sec")
    req_count = lax.axis_size("req")
    req_id = lax.axis_index("req")
    rows = prompt_x.shape[0] // sec_count
    width = w_kv.shape[1]

    def over(value, sec_flip, req_flip):
        if req_flip == 0:
            return lax.ppermute(value, "sec", [(i, i ^ sec_flip) for i in range(sec_count)])
        if sec_flip == 0:
            return lax.ppermute(value, "req", [(i, i ^ req_flip) for i in range(req_count)])
        return over_cores(value, (sec_flip, req_flip), (sec_flip, req_flip))

    def over_cores(value, flips_0, flips_1):
        pairs = []
        for i in range(sec_count):
            for j in range(req_count):
                sec_flip, req_flip = flips_1 if j % 2 else flips_0
                pairs.append((i * req_count + j, (i ^ sec_flip) * req_count + (j ^ req_flip)))
        return lax.ppermute(value, ("sec", "req"), pairs)

    chunk = shape((rows, width), BF)
    everyone = shape((NREQ, queries.shape[1]), BF)
    other_queries = over(queries, 0, 1)
    gathered = call(
        place_mine_kernel, [(vmem(), queries)], everyone, "place_mine", flops=2_000_000_000
    )
    gathered = call(
        place_other_kernel, [(vmem(), gathered), (vmem(), other_queries)], everyone, "place_other"
    )
    gathered = gathered + over(gathered, 0, 2)
    chunks = call(
        kv_kernel,
        [(vmem(), prompt_x), (vmem(), w_kv)],
        (chunk, chunk, chunk, chunk),
        "new_kv",
        flops=2 * prompt_x.size * width,
    )
    arrived = [over(chunks[flip], flip, 0) for flip in (3, 2, 1)]
    gathered = gathered + over(gathered, 0, 6)
    cached_weighted, cached_stats, live = call(
        cached_kernel,
        [
            (vmem(), blk_owner.reshape(1, -1)),
            (vmem(), blk_slot.reshape(1, -1)),
            (vmem(), blk_len.reshape(1, -1)),
            (vmem(), ctx_len.reshape(1, -1)),
            (vmem(), queries),
            (vmem(), cache[:, :, 0, :]),
        ],
        (shape((HD, LANES), F32), shape((8, LANES), F32), shape((rows, LANES), F32)),
        "cached",
        flops=2 * 4 * cache.shape[1] * HD * LANES,
    )
    new_kv = call(
        sum_kernel, [(vmem(), value) for value in (chunks[0], *arrived)], chunk, "kv_sum"
    )
    kept = call(
        prompt_kernel,
        [
            (vmem(), value)
            for value in (gathered, live, new_kv, cached_weighted, cached_stats)
        ],
        STATE,
        "prompt",
        flops=2 * 2 * rows * HD * LANES,
    )
    for name, moves in (
        ("join_core", ((0, 1),)),
        ("join_near", ((0, 2), (0, 6), (0, 4))),
    ):
        got = [over(kept[2], *flips) for flips in moves]
        kept = call(
            join_kernel, [(vmem(), value) for value in (kept[0], kept[1], *got)], STATE, name
        )
    got = [
        over_cores(kept[2], own, flips) for own, flips in (((1, 0), (3, 0)), ((0, 2), (2, 0)))
    ]
    far = call(far_kernel, [(vmem(), value) for value in got], STATE, "join_far")
    columns = w_out.shape[1]
    partial_out = call(
        project_kernel,
        [
            (vmem(), value)
            for value in (kept[0], kept[1], far[0], far[1], w_out, over(far[2], 0, 1))
        ],
        shape((NREQ, columns), BF),
        "project",
        flops=2 * w_out.size * NREQ,
    )
    head_count = lax.axis_size("head")
    pieces = partial_out.reshape(head_count, NREQ // head_count, columns)
    pieces = lax.all_to_all(pieces, "head", 0, 0, tiled=True)
    return jnp.sum(pieces.astype(F32), axis=0).astype(BF)


def solution(mesh):
    return jax.shard_map(
        on_device,
        mesh=mesh,
        in_specs=(
            P("req", "sec"),
            P("sec", "head"),
            P("req", "head"),
            P("req", "sec", "head", None),
            P("head", ("sec", "req")),
            P(),
            P(),
            P(),
            P("req"),
        ),
        out_specs=P("head", ("sec", "req")),
        check_vma=False,
    )
```

```python
import math

import jax
import jax.numpy as jnp
from jax import lax
from jax.experimental import pallas as pl
from jax.experimental.pallas import tpu as pltpu
from jax.sharding import PartitionSpec as P

HD = 128
BLK = 16
GROUP = 16
NREQ = 16
LANES = GROUP * NREQ
STAT = 16
LOW = -1e30
FACTOR = 1.0 / math.sqrt(HD)
BF = jnp.bfloat16
F32 = jnp.float32


def vmem():
    return pl.BlockSpec(memory_space=pltpu.VMEM)


def dot(a, b, dims):
    return lax.dot_general(a, b, (dims, ((), ())), preferred_element_type=F32)


def rows_of(queries):
    return jnp.concatenate([queries[:, h * HD : (h + 1) * HD] for h in range(GROUP)], axis=0)


def stat_rows(peak, total, rows):
    place = lax.broadcasted_iota(jnp.int32, (rows, peak.shape[1]), 0)
    return jnp.where(place == 0, peak, jnp.where(place == 1, total, 0.0))


def packed_stats(peak, total):
    hi = peak.astype(BF).astype(F32)
    rest = peak - hi
    mid = rest.astype(BF).astype(F32)
    low = rest - mid
    total_hi = total.astype(BF).astype(F32)
    total_low = total - total_hi
    place = lax.broadcasted_iota(jnp.int32, (STAT, peak.shape[1]), 0)
    packed = jnp.zeros((STAT, peak.shape[1]), F32)
    for row, part in enumerate((hi, mid, low, total_hi, total_low)):
        packed = jnp.where(place == row, part, packed)
    return packed.astype(BF)


def unpacked_stats(packed):
    rows = packed.astype(F32)
    peak = rows[0:1] + (rows[1:2] + rows[2:3])
    total = rows[3:4] + rows[4:5]
    return peak, total


def store_packed(ref, weighted, peak, total):
    ref[0:HD, :] = weighted.astype(BF)
    ref[HD : HD + STAT, :] = packed_stats(peak, total)


def kv_kernel(x_ref, w_ref, out0, out1, out2, out3):
    sec_id = lax.axis_index("sec")
    rows = out0.shape[0]
    for flip, out in enumerate((out0, out1, out2, out3)):
        start = pl.multiple_of((sec_id ^ flip) * rows, rows)
        out[...] = dot(x_ref[pl.ds(start, rows), :], w_ref[...], ((1,), (0,))).astype(BF)


def sum_kernel(own_ref, a_ref, b_ref, c_ref, out_ref):
    summed = (own_ref[...].astype(F32) + a_ref[...].astype(F32)) + (
        b_ref[...].astype(F32) + c_ref[...].astype(F32)
    )
    out_ref[...] = summed.astype(BF)


def cached_kernel(
    owner_ref, slot_ref, len_ref, ctx_ref, q_ref, cache_ref, weighted_ref, stats_ref, live_ref
):
    sec_id, req_id = lax.axis_index("sec"), lax.axis_index("req")
    count = cache_ref.shape[1]
    position = lax.broadcasted_iota(jnp.int32, (GROUP, count), 1) + sec_id * count
    lane = lax.broadcasted_iota(jnp.int32, (GROUP, LANES), 1)
    head = lax.broadcasted_iota(jnp.int32, (GROUP, LANES), 0)
    weighted = jnp.zeros((HD, LANES), F32)
    peaks = jnp.full((1, LANES), LOW, F32)
    totals = jnp.zeros((1, LANES), F32)
    for slot in range(2):
        queries = jnp.concatenate(
            [q_ref[slot : slot + 1, h * HD : (h + 1) * HD] for h in range(GROUP)], axis=0
        )
        live = position < ctx_ref[0:1, slot : slot + 1]
        scores = dot(queries, cache_ref[slot, :, 0:HD], ((1,), (1,))) * FACTOR
        scores = jnp.where(live, scores, LOW)
        peak = jnp.max(scores, axis=1, keepdims=True)
        weights = jnp.where(live, jnp.exp(scores - peak), 0.0)
        total = jnp.sum(weights, axis=1, keepdims=True)
        summed = dot(weights.astype(BF), cache_ref[slot, :, HD : 2 * HD], ((1,), (0,)))
        lane_of = lane == head * NREQ + req_id * 2 + slot
        spread = lane_of.astype(BF)
        high = summed.astype(BF)
        low = (summed - high.astype(F32)).astype(BF)
        weighted = weighted + dot(high, spread, ((0,), (0,))) + dot(low, spread, ((0,), (0,)))
        peaks = jnp.maximum(
            peaks, jnp.max(jnp.where(lane_of, peak, LOW), axis=0, keepdims=True)
        )
        totals = totals + jnp.sum(jnp.where(lane_of, total, 0.0), axis=0, keepdims=True)
    weighted_ref[...] = weighted
    stats_ref[...] = stat_rows(peaks, totals, 8)

    rows, blocks = live_ref.shape[0], owner_ref.shape[1]
    first = (req_id * lax.axis_size("sec") + sec_id) * (rows // BLK)
    token = lax.broadcasted_iota(jnp.int32, (rows, blocks), 0)
    block = lax.broadcasted_iota(jnp.int32, (rows, blocks), 1)
    mine = block == token // BLK + first
    holder = owner_ref[...] * 2 + slot_ref[...]
    holder = jnp.sum(jnp.where(mine, holder, 0).astype(F32), axis=1, keepdims=True)
    length = jnp.sum(jnp.where(mine, len_ref[...], 0).astype(F32), axis=1, keepdims=True)
    lane = lax.broadcasted_iota(jnp.int32, (rows, LANES), 1) % NREQ
    place = lax.broadcasted_iota(jnp.int32, (rows, LANES), 0) % BLK
    live = (lane.astype(F32) == holder) & (place.astype(F32) < length)
    live_ref[...] = live.astype(F32)


def placed(rows, holder):
    place = lax.broadcasted_iota(jnp.int32, (NREQ, 2), 0)
    row = lax.broadcasted_iota(jnp.int32, (NREQ, 2), 1)
    return dot((place == holder * 2 + row).astype(BF), rows, ((1,), (0,)))


def place_mine_kernel(mine_ref, out_ref):
    out_ref[...] = placed(mine_ref[...], lax.axis_index("req")).astype(BF)


def place_other_kernel(so_far_ref, other_ref, out_ref):
    other = placed(other_ref[...], lax.axis_index("req") ^ 1)
    out_ref[...] = (so_far_ref[...].astype(F32) + other).astype(BF)


def prompt_kernel(q_ref, live_ref, kv_ref, cw_ref, cs_ref, kw_ref, ks_ref, send_ref):
    new_kv = kv_ref[...]
    queries = rows_of(q_ref[...])
    live = live_ref[...] > 0.5
    scores = dot(new_kv[:, 0:HD], queries, ((1,), (1,))) * FACTOR
    scores = jnp.where(live, scores, LOW)
    peak = jnp.max(scores, axis=0, keepdims=True)
    weights = jnp.where(live, jnp.exp(scores - peak), 0.0)
    total = jnp.sum(weights, axis=0, keepdims=True)
    weighted = dot(new_kv[:, HD : 2 * HD], weights.astype(BF), ((0,), (0,)))
    cached_peak, cached_total = cs_ref[0:1, :], cs_ref[1:2, :]
    joint = jnp.maximum(peak, cached_peak)
    scale, cached_scale = jnp.exp(peak - joint), jnp.exp(cached_peak - joint)
    weighted = weighted * scale + cw_ref[...] * cached_scale
    total = total * scale + cached_total * cached_scale
    kw_ref[...] = weighted
    ks_ref[...] = stat_rows(joint, total, 8)
    store_packed(send_ref, weighted, joint, total)


def joined(w_ref, s_ref, got_refs):
    peaks, totals = [s_ref[0:1, :]], [s_ref[1:2, :]]
    for got_ref in got_refs:
        peak, total = unpacked_stats(got_ref[HD : HD + STAT, :])
        peaks.append(peak)
        totals.append(total)
    joint = peaks[0]
    for peak in peaks[1:]:
        joint = jnp.maximum(joint, peak)
    scales = [jnp.exp(peak - joint) for peak in peaks]
    weighted, total = w_ref[...] * scales[0], totals[0] * scales[0]
    for got_ref, part, scale in zip(got_refs, totals[1:], scales[1:]):
        weighted = weighted + got_ref[0:HD, :].astype(F32) * scale
        total = total + part * scale
    return weighted, joint, total


def join_kernel(w_ref, s_ref, *refs):
    got_refs, (kw_ref, ks_ref, send_ref) = refs[:-3], refs[-3:]
    weighted, peak, total = joined(w_ref, s_ref, got_refs)
    kw_ref[...] = weighted
    ks_ref[...] = stat_rows(peak, total, 8)
    store_packed(send_ref, weighted, peak, total)


def far_kernel(first_ref, second_ref, kw_ref, ks_ref, send_ref):
    use_second = (lax.axis_index("req") % 2).astype(F32)
    peak, total = unpacked_stats(first_ref[HD : HD + STAT, :])
    peak_2, total_2 = unpacked_stats(second_ref[HD : HD + STAT, :])
    joint = jnp.maximum(peak, peak_2)
    scale, scale_2 = jnp.exp(peak - joint), jnp.exp(peak_2 - joint) * use_second
    weighted = first_ref[0:HD, :].astype(F32) * scale + second_ref[0:HD, :].astype(F32) * scale_2
    total = total * scale + total_2 * scale_2
    kw_ref[...] = weighted
    ks_ref[...] = stat_rows(joint, total, 8)
    store_packed(send_ref, weighted, joint, total)


def project_kernel(w_ref, s_ref, far_w_ref, far_s_ref, out_w_ref, got_ref, out_ref):
    weighted, peak, total = joined(w_ref, s_ref, (got_ref,))
    far_peak, far_total = far_s_ref[0:1, :], far_s_ref[1:2, :]
    joint = jnp.maximum(peak, far_peak)
    scale, far_scale = jnp.exp(peak - joint), jnp.exp(far_peak - joint)
    weighted = weighted * scale + far_w_ref[...] * far_scale
    total = total * scale + far_total * far_scale
    rows = (weighted / total).T.astype(BF)
    attended = jnp.concatenate(
        [rows[h * NREQ : (h + 1) * NREQ, :] for h in range(GROUP)], axis=1
    )
    out_ref[...] = dot(attended, out_w_ref[...], ((1,), (0,))).astype(BF)


def shape(dims, dtype):
    return jax.ShapeDtypeStruct(dims, dtype)


def call(kernel, ins, outs, name, flops=0, scratch=(), grant=32):
    moved = 0
    for _, value in ins:
        moved += value.size * value.dtype.itemsize
    return pl.pallas_call(
        kernel,
        out_shape=outs,
        in_specs=[spec for spec, _ in ins],
        out_specs=jax.tree.map(lambda _: vmem(), outs),
        scratch_shapes=scratch,
        compiler_params=pltpu.CompilerParams(vmem_limit_bytes=grant * 1024 * 1024),
        cost_estimate=pl.CostEstimate(flops=flops, bytes_accessed=moved, transcendentals=0),
        name=name,
    )(*[value for _, value in ins])


STATE = (shape((HD, LANES), F32), shape((8, LANES), F32), shape((HD + STAT, LANES), BF))


def on_device(prompt_x, w_kv, queries, cache, w_out, blk_owner, blk_slot, blk_len, ctx_len):
    sec_count = lax.axis_size("sec")
    req_count = lax.axis_size("req")
    req_id = lax.axis_index("req")
    rows = prompt_x.shape[0] // sec_count
    width = w_kv.shape[1]

    def over(value, sec_flip, req_flip):
        if req_flip == 0:
            return lax.ppermute(value, "sec", [(i, i ^ sec_flip) for i in range(sec_count)])
        if sec_flip == 0:
            return lax.ppermute(value, "req", [(i, i ^ req_flip) for i in range(req_count)])
        return over_cores(value, (sec_flip, req_flip), (sec_flip, req_flip))

    def over_cores(value, flips_0, flips_1):
        pairs = []
        for i in range(sec_count):
            for j in range(req_count):
                sec_flip, req_flip = flips_1 if j % 2 else flips_0
                pairs.append((i * req_count + j, (i ^ sec_flip) * req_count + (j ^ req_flip)))
        return lax.ppermute(value, ("sec", "req"), pairs)

    chunk = shape((rows, width), BF)
    everyone = shape((NREQ, queries.shape[1]), BF)
    other_queries = over(queries, 0, 1)
    gathered = call(
        place_mine_kernel, [(vmem(), queries)], everyone, "place_mine", flops=2_000_000_000
    )
    gathered = call(
        place_other_kernel, [(vmem(), gathered), (vmem(), other_queries)], everyone, "place_other"
    )
    gathered = gathered + over(gathered, 0, 2)
    chunks = call(
        kv_kernel,
        [(vmem(), prompt_x), (vmem(), w_kv)],
        (chunk, chunk, chunk, chunk),
        "new_kv",
        flops=2 * prompt_x.size * width,
    )
    arrived = [over(chunks[flip], flip, 0) for flip in (3, 1, 2)]
    gathered = gathered + over(gathered, 0, 6)
    cached_weighted, cached_stats, live = call(
        cached_kernel,
        [
            (vmem(), blk_owner.reshape(1, -1)),
            (vmem(), blk_slot.reshape(1, -1)),
            (vmem(), blk_len.reshape(1, -1)),
            (vmem(), ctx_len.reshape(1, -1)),
            (vmem(), queries),
            (vmem(), cache[:, :, 0, :]),
        ],
        (shape((HD, LANES), F32), shape((8, LANES), F32), shape((rows, LANES), F32)),
        "cached",
        flops=2 * 4 * cache.shape[1] * HD * LANES,
    )
    new_kv = call(
        sum_kernel, [(vmem(), value) for value in (chunks[0], *arrived)], chunk, "kv_sum"
    )
    kept = call(
        prompt_kernel,
        [
            (vmem(), value)
            for value in (gathered, live, new_kv, cached_weighted, cached_stats)
        ],
        STATE,
        "prompt",
        flops=2 * 2 * rows * HD * LANES,
    )
    for name, moves in (
        ("join_core", ((0, 1),)),
        ("join_near", ((0, 2), (0, 6), (0, 4))),
    ):
        got = [over(kept[2], *flips) for flips in moves]
        kept = call(
            join_kernel, [(vmem(), value) for value in (kept[0], kept[1], *got)], STATE, name
        )
    got = [
        over_cores(kept[2], own, flips) for own, flips in (((1, 0), (3, 0)), ((0, 2), (2, 0)))
    ]
    far = call(far_kernel, [(vmem(), value) for value in got], STATE, "join_far")
    columns = w_out.shape[1]
    partial_out = call(
        project_kernel,
        [
            (vmem(), value)
            for value in (kept[0], kept[1], far[0], far[1], w_out, over(far[2], 0, 1))
        ],
        shape((NREQ, columns), BF),
        "project",
        flops=2 * w_out.size * NREQ,
    )
    head_count = lax.axis_size("head")
    pieces = partial_out.reshape(head_count, NREQ // head_count, columns)
    pieces = lax.all_to_all(pieces, "head", 0, 0, tiled=True)
    return jnp.sum(pieces.astype(F32), axis=0).astype(BF)


def solution(mesh):
    return jax.shard_map(
        on_device,
        mesh=mesh,
        in_specs=(
            P("req", "sec"),
            P("sec", "head"),
            P("req", "head"),
            P("req", "sec", "head", None),
            P("head", ("sec", "req")),
            P(),
            P(),
            P(),
            P("req"),
        ),
        out_specs=P("head", ("sec", "req")),
        check_vma=False,
    )
```
